128 devices in a mesh: section: 8 (over y_hi, x), seq: 16 (over y_lo, z, core).
Axes of the slice: x: 4, y: 4 (y_hi: 2, y_lo: 2; y = y_hi * 2 + y_lo), z: 4, core: 2. Of those that a mesh axis runs over, the one named last changes fastest.
Arguments:
- video: bfloat16 [8, 2048, 3072], P('section', 'seq'), may hold values from -6 to 6
- text: bfloat16 [8, 128, 3072], P('section', 'seq'), may hold values from -6 to 6
- prompt_len: int32 [8], P('section'), may hold values from 1 to 128, as said below
- modulation: float32 [8, 3, 3072], P('section'), may hold values from -3 to 3
- q_gain: float32 [128], replicated, may hold values from 0.5 to 2
- k_gain: float32 [128], replicated, may hold values from 0.5 to 2
- w_qkv: bfloat16 [3072, 3, 2048], P(None, None, 'seq'), may hold values from -0.109375 to 0.109375
- w_out: bfloat16 [2048, 3072], replicated, may hold values from -0.125 to 0.125
- cot_video: bfloat16 [8, 2048, 3072], P('section', 'seq'), may hold values from -6 to 6
- cot_text: bfloat16 [8, 128, 3072], P('section', 'seq'), may hold values from -6 to 6
Outputs:
- video_out: bfloat16 [8, 2048, 3072], P('section', 'seq')
- text_out: bfloat16 [8, 128, 3072], P('section', 'seq')
- grad_video: bfloat16 [8, 2048, 3072], P('section', 'seq')
- grad_text: bfloat16 [8, 128, 3072], P('section', 'seq')
- grad_modulation: float32 [8, 3, 3072], P('section')
- grad_wqkv: float32 [3072, 3, 2048], P('section', None, 'seq')
- grad_gains: float32 [2, 128], replicated
The draws below stay inside these ranges and needn't reach their ends.
Inputs may be any that keep to these rules, and one draw needn't show every extreme that they name: `prompt_len`: some sample uses all 128 text rows.
All inputs are finite; a program needn't handle non-finite values.
Results may differ from the reference program's by a relative error of at most 0.019.
Values may be sent and summed in bfloat16 or wider, within the bound.
No kernel may reach another device: no remote copies, remote signals or barrier semaphores. Data moves between devices by JAX's collectives and lax.ppermute only.
A program may use at most 192 MiB of HBM per device.

```python
import math
import jax
import jax.numpy as jnp
from jax import lax

D = 3072
HEAD_DIM = 128
HEADS = 16
SAMPLES = 8
VID = 2048
TXT = 128
N_SEQ = 16


def draw_prompt_len(key, part):
    key = jax.random.fold_in(key, 7)
    first, second = jax.random.split(key)
    lengths = jax.random.randint(first, (SAMPLES,), 1, TXT + 1, dtype=jnp.int32)
    chosen = jax.random.randint(second, (), 0, SAMPLES, dtype=jnp.int32)
    return jnp.where(jnp.arange(SAMPLES, dtype=jnp.int32) == chosen, jnp.int32(TXT), lengths)


def block_levels(own_key, extent, cuts, low, largest):
    def one(axis_at, blocks):
        heights = jax.random.uniform(jax.random.fold_in(jax.random.fold_in(own_key, 6), axis_at), (blocks,), jnp.float32, low / len(cuts), largest / len(cuts))
        return jnp.repeat(jnp.exp(heights), extent[axis_at] // blocks).reshape((-1,) + (1,) * (len(extent) - axis_at - 1))

    level = one(*cuts[0])
    for cut in cuts[1:]:
        level = level * one(*cut)
    return level


def gaussian(own_key, extent, scale, bound, pieces=(), kind=jnp.bfloat16):
    values = scale * jax.random.normal(own_key, extent, jnp.float32)
    if pieces:
        values = values * block_levels(own_key, extent, pieces, -0.22, 0.18)
    return jnp.clip(values, -bound, bound).astype(kind)


def setup_inputs(seed: int = 0) -> dict:
    splits = jax.random.split(jax.random.key(seed), 11)
    return {
        "video": gaussian(splits[0], (SAMPLES, VID, D), 1.0, 6.0, ((0, 8), (1, 16))),
        "text": gaussian(splits[1], (SAMPLES, TXT, D), 1.0, 6.0, ((0, 8), (1, 16))),
        "prompt_len": draw_prompt_len(jax.random.fold_in(splits[10], 71), 0),
        "modulation": gaussian(splits[3], (SAMPLES, 3, D), 0.5, 3.0, ((0, 8),), jnp.float32),
        "q_gain": jnp.clip(jnp.exp(jax.random.uniform(splits[4], (HEAD_DIM,), jnp.float32, math.log(0.5), math.log(2.0))), 0.5, 2.0),
        "k_gain": jnp.clip(jnp.exp(jax.random.uniform(splits[5], (HEAD_DIM,), jnp.float32, math.log(0.5), math.log(2.0))), 0.5, 2.0),
        "w_qkv": gaussian(splits[6], (D, 3, HEADS * HEAD_DIM), D ** -0.5, 0.109375, ((2, 16),)),
        "w_out": gaussian(splits[7], (HEADS * HEAD_DIM, D), (HEADS * HEAD_DIM) ** -0.5, 0.125),
        "cot_video": gaussian(splits[8], (SAMPLES, VID, D), 1.0, 6.0, ((0, 8), (1, 16))),
        "cot_text": gaussian(splits[9], (SAMPLES, TXT, D), 1.0, 6.0, ((0, 8), (1, 16))),
    }


def layer_norm(values):
    center = values - lax.optimization_barrier(jnp.mean(values, axis=-1, keepdims=True))
    return center * lax.rsqrt(lax.optimization_barrier(jnp.mean(center * center, axis=-1, keepdims=True)) + 1e-06)

def rms_scale(values, gain):
    return values * lax.rsqrt(lax.optimization_barrier(jnp.mean(values * values, axis=-1, keepdims=True)) + 1e-06) * gain

def prepare(q_raw, k_raw, v_raw, q_gain, k_gain):
    q_norm = (rms_scale(q_raw, q_gain) * q_raw.shape[-1] ** (-0.5)).astype(jnp.bfloat16)
    k_norm = rms_scale(k_raw, k_gain).astype(jnp.bfloat16)
    return (q_norm, k_norm, v_raw.astype(jnp.bfloat16))

def head_attend(query, keys, values, bias):
    scores = jnp.dot(query, keys.T, preferred_element_type=jnp.float32) + bias[None, :]
    scores = scores - lax.optimization_barrier(jnp.max(scores, axis=-1, keepdims=True))
    expo = jnp.exp(scores)
    weights = (expo / lax.optimization_barrier(jnp.sum(expo, axis=-1, keepdims=True))).astype(jnp.bfloat16)
    return jnp.dot(weights, values, preferred_element_type=jnp.float32)

def attend(queries, keys, values, bias):
    single = jax.checkpoint(lambda items: head_attend(items[0], items[1], items[2], bias))
    return lax.map(single, (queries, keys, values))

def reference(video, text, prompt_len, modulation, q_gain, k_gain, w_qkv, w_out, cot_video, cot_text):
    width = video.shape[2]
    per_head = q_gain.shape[0]
    head_cols = w_qkv.shape[2]
    heads = head_cols // per_head
    nall = VID + TXT
    w_flat = w_qkv.reshape(width, 3 * head_cols)
    grad_w = jnp.zeros((width, 3 * head_cols), jnp.float32)
    grad_gain = jnp.zeros((2, per_head), jnp.float32)
    outs_v, outs_t, grads_v, grads_t, grads_m = ([], [], [], [], [])
    for sample in range(SAMPLES):
        joined = jnp.concatenate([video[sample], text[sample]], axis=0).astype(jnp.float32)
        shift, scale, gate = (modulation[sample, 0], modulation[sample, 1], modulation[sample, 2])
        normed, norm_back = jax.vjp(layer_norm, joined)
        h = (normed * (1.0 + scale) + shift).astype(jnp.bfloat16)
        qkv = jnp.dot(h, w_flat, preferred_element_type=jnp.float32).reshape(nall, 3, heads, per_head)
        (q_norm, k_norm, v_norm), prep_back = jax.vjp(prepare, qkv[:, 0], qkv[:, 1], qkv[:, 2], q_gain, k_gain)
        position = jnp.arange(nall, dtype=jnp.int32)
        valid = (position < VID) | (position - VID < prompt_len[sample])
        bias = jnp.where(valid, 0.0, -1e+30).astype(jnp.float32)
        attn_fn = lambda qa, ka, va: attend(qa, ka, va, bias)
        attn_heads, attn_back = jax.vjp(attn_fn, jnp.transpose(q_norm, (1, 0, 2)), jnp.transpose(k_norm, (1, 0, 2)), jnp.transpose(v_norm, (1, 0, 2)))
        attn = jnp.transpose(attn_heads, (1, 0, 2)).reshape(nall, head_cols).astype(jnp.bfloat16)
        out = jnp.dot(attn, w_out, preferred_element_type=jnp.float32)
        result = (joined + gate * out).astype(jnp.bfloat16)
        dy = jnp.concatenate([cot_video[sample], cot_text[sample]], axis=0).astype(jnp.float32)
        d_out = (dy * gate).astype(jnp.bfloat16)
        d_attn = jnp.dot(d_out, w_out.T, preferred_element_type=jnp.float32).astype(jnp.bfloat16)
        d_heads = jnp.transpose(d_attn.astype(jnp.float32).reshape(nall, heads, per_head), (1, 0, 2))
        dq, dk, dv = attn_back(d_heads)
        dq, dk, dv = (jnp.transpose(dq, (1, 0, 2)), jnp.transpose(dk, (1, 0, 2)), jnp.transpose(dv, (1, 0, 2)))
        dq_raw, dk_raw, dv_raw, dgq, dgk = prep_back((dq, dk, dv))
        d_qkv = jnp.stack([dq_raw, dk_raw, dv_raw], axis=1).reshape(nall, 3, head_cols).astype(jnp.bfloat16)
        grad_w = grad_w + jnp.dot(h.T, d_qkv.reshape(nall, 3 * head_cols), preferred_element_type=jnp.float32)
        grad_gain = grad_gain + jnp.stack([dgq, dgk], axis=0)
        group_cols = head_cols // N_SEQ
        d_h = jnp.zeros((nall, width), jnp.float32)
        for group in range(N_SEQ):
            piece = d_qkv[:, :, group * group_cols:(group + 1) * group_cols].reshape(nall, 3 * group_cols)
            wpiece = w_qkv[:, :, group * group_cols:(group + 1) * group_cols].reshape(width, 3 * group_cols)
            part = jnp.dot(piece, wpiece.T, preferred_element_type=jnp.float32).astype(jnp.bfloat16)
            d_h = d_h + part.astype(jnp.float32)
        d_joined = (dy + norm_back(d_h * (1.0 + scale))[0]).astype(jnp.bfloat16)
        grads_m.append(jnp.stack([lax.optimization_barrier(jnp.sum(d_h, axis=0)), lax.optimization_barrier(jnp.sum(d_h * normed, axis=0)), lax.optimization_barrier(jnp.sum(dy * out, axis=0))], axis=0))
        outs_v.append(result[:VID])
        outs_t.append(result[VID:])
        grads_v.append(d_joined[:VID])
        grads_t.append(d_joined[VID:])
    return (jnp.stack(outs_v), jnp.stack(outs_t), jnp.stack(grads_v), jnp.stack(grads_t), jnp.stack(grads_m), grad_w.reshape(width, 3, head_cols), grad_gain)
```

```python
import functools
import jax
import jax.numpy as jnp
from jax import lax
from jax.experimental import pallas as pl
from jax.experimental.pallas import tpu as pltpu
from jax.sharding import Mesh
from jax.sharding import PartitionSpec as P

BF=jnp.bfloat16; F=jnp.float32
HD=128

def attn_kernel(block, chunk, order_ref, own_ref, sib_ref, bias_ref, do_ref, gq_ref, gk_ref,
                attn_ref, dqkv_ref, gain_ref, kn_s, v_s, dk_s, dv_s):
    half=own_ref.shape[0]
    n=2*half
    scale=HD**-0.5
    step=pl.program_id(0)
    per=block//chunk
    gq=gq_ref[...]; gk=gk_ref[...]
    def norm(x):
        r=lax.rsqrt(jnp.mean(x*x,axis=-1,keepdims=True)+1e-6)
        return x*r, r
    @pl.when(step==0)
    def _():
        for ref,at in ((own_ref,0),(sib_ref,half)):
            x=ref[:,HD:2*HD].astype(F)
            xh,_r=norm(x)
            kn_s[at:at+half,:]=(xh*gk).astype(BF)
            v_s[at:at+half,:]=ref[:,2*HD:]
        dk_s[...]=jnp.zeros_like(dk_s); dv_s[...]=jnp.zeros_like(dv_s)
        gain_ref[...]=jnp.zeros_like(gain_ref)
    nh=half//block
    def body(ref,row):
        rows=pl.ds(pl.multiple_of(row,16),block)
        x=ref[rows,0:HD].astype(F)
        xh,r=norm(x)
        qn=(xh*(gq*scale)).astype(BF)
        s=lax.dot_general(qn,kn_s[...],(((1,),(1,)),((),())),preferred_element_type=F)+bias_ref[...]
        e=jnp.exp(s)
        linv=1.0/jnp.sum(e,axis=-1,keepdims=True)
        eb=e.astype(BF)
        o=jnp.dot(eb,v_s[...],preferred_element_type=F)*linv
        do=jnp.concatenate([do_ref[order_ref[step*per+j]].astype(F) for j in range(per)],axis=0)
        ob=o.astype(BF)
        for j in range(per):
            attn_ref[order_ref[step*per+j]]=o[j*chunk:(j+1)*chunk].astype(BF)
        dn=do*linv
        dnb=dn.astype(BF)
        delta=jnp.sum(dn*o,axis=-1,keepdims=True)
        dp=lax.dot_general(dnb,v_s[...],(((1,),(1,)),((),())),preferred_element_type=F)
        ds=(e*(dp-delta)).astype(BF)
        dq=jnp.dot(ds,kn_s[...],preferred_element_type=F)
        dk_s[...]+=lax.dot_general(ds,qn,(((0,),(0,)),((),())),preferred_element_type=F)
        dv_s[...]+=lax.dot_general(eb,dnb,(((0,),(0,)),((),())),preferred_element_type=F)
        t=dq*(gq*scale)
        dx=r*(t-xh*jnp.mean(t*xh,axis=-1,keepdims=True))
        gain_ref[0:1,:]+=jnp.sum(dq*xh,axis=0,keepdims=True)*scale
        return dx
    @pl.when(step<nh)
    def _():
        dx=body(own_ref,step*block)
        dqkv_ref[pl.ds(pl.multiple_of(step*block,16),block),0:HD]=dx.astype(BF)
    @pl.when(step>=nh)
    def _():
        dx=body(sib_ref,(step-nh)*block)
        dqkv_ref[pl.ds(pl.multiple_of(step*block,16),block),0:HD]=dx.astype(BF)
    @pl.when(step==2*nh-1)
    def _():
        for ref,at in ((own_ref,0),(sib_ref,half)):
            x=ref[:,HD:2*HD].astype(F)
            xh,r=norm(x)
            dk=dk_s[at:at+half,:]
            t=dk*gk
            dx=r*(t-xh*jnp.mean(t*xh,axis=-1,keepdims=True))
            gain_ref[1:2,:]+=jnp.sum(dk*xh,axis=0,keepdims=True)
            dqkv_ref[at:at+half,HD:2*HD]=dx.astype(BF)
            dqkv_ref[at:at+half,2*HD:]=dv_s[at:at+half,:].astype(BF)

def attention(order, own, sib, bias, do, gq, gk, block=544):
    half=own.shape[0]; n=2*half; chunk=do.shape[1]
    full=lambda shape: pl.BlockSpec(shape,lambda i,o: (0,)*len(shape))
    return pl.pallas_call(
        functools.partial(attn_kernel,block,chunk),
        out_shape=(jax.ShapeDtypeStruct(do.shape,BF),jax.ShapeDtypeStruct((n,3*HD),BF),jax.ShapeDtypeStruct((2,HD),F)),
        grid_spec=pltpu.PrefetchScalarGridSpec(
            num_scalar_prefetch=1, grid=(n//block,),
            in_specs=[full((half,3*HD)),full((half,3*HD)),full((1,n)),full(do.shape),full((1,HD)),full((1,HD))],
            out_specs=[full(do.shape),full((n,3*HD)),full((2,HD))],
            scratch_shapes=[pltpu.VMEM((n,HD),BF),pltpu.VMEM((n,HD),BF),pltpu.VMEM((n,HD),F),pltpu.VMEM((n,HD),F)]),
        compiler_params=pltpu.CompilerParams(vmem_limit_bytes=56*2**20),
        cost_estimate=pl.CostEstimate(flops=12*n*n*HD,bytes_accessed=n*HD*20,transcendentals=n*n),
    )(order,own,sib,bias,do,gq,gk)


SEQ = ("y", "z", "core")
SECTION = ("yh", "x")
EVERY = SECTION + SEQ


def ring(values, axis, distance):
    size = lax.axis_size(axis)
    return lax.ppermute(values, axis, [(i, (i + distance) % size) for i in range(size)])


def per_device(
    video, text, prompt_len, modulation, q_gain, k_gain, w_qkv, w_out, cot_video, cot_text
):
    vrows, trows = video.shape[1], text.shape[1]
    rows = vrows + trows
    width = video.shape[2]
    per_head = q_gain.shape[0]
    heads = w_out.shape[0] // per_head
    cols = 3 * per_head
    yi, zi, ci = (lax.axis_index(a) for a in SEQ)
    zp = functools.partial(ring, axis="z", distance=1)
    zm = functools.partial(ring, axis="z", distance=-1)
    yy = functools.partial(ring, axis="y", distance=1)
    cc = functools.partial(ring, axis="core", distance=1)
    shift, scale, gate = (modulation[0, 0], modulation[0, 1], modulation[0, 2])
    joined = jnp.concatenate([video[0], text[0]], axis=0).astype(F)
    center = joined - jnp.mean(joined, axis=-1, keepdims=True)
    rstd = lax.rsqrt(jnp.mean(center * center, axis=-1, keepdims=True) + 1e-06)
    normed = center * rstd
    h = (normed * (1.0 + scale) + shift).astype(BF)

    cut = (rows * 10 // 17) // 8 * 8
    mid = cut // 16 * 8
    half = (rows // 2 + 7) // 8 * 8
    h_y = yy(h)
    h_a = zp(h)
    h_b = zm(h)
    h_c = jnp.concatenate([zp(h_a[:half]), zm(h_b[half:])], axis=0)
    d_a = zp(h_y[:cut])
    d_b = zm(h_y[:cut])
    h_ya = jnp.concatenate([d_a, yy(h_a[cut:])], axis=0)
    h_yb = jnp.concatenate([d_b, yy(h_b[cut:])], axis=0)
    h_yc = jnp.concatenate([zp(d_a[:mid]), zm(d_b[mid:]), yy(h_c[cut:])], axis=0)
    w_own = w_qkv.reshape(width, cols)
    w_both = jnp.concatenate([w_own, cc(w_own)], axis=1)
    h_one = jnp.concatenate([h, h_y, h_a, h_b], axis=0)
    h_two = jnp.concatenate([h_c, h_ya, h_yb, h_yc], axis=0)
    qkv_one = jnp.dot(h_one, w_both, preferred_element_type=F).astype(BF)
    qkv_two = jnp.dot(h_two, w_both, preferred_element_type=F).astype(BF)
    own = jnp.concatenate([qkv_one[:, :cols], qkv_two[:, :cols]], axis=0)
    sib = jnp.concatenate([cc(qkv_one[:, cols:]), cc(qkv_two[:, cols:])], axis=0)

    dy = jnp.concatenate([cot_video[0], cot_text[0]], axis=0).astype(F)
    d_out = (dy * gate).astype(BF)
    w_heads = w_out.reshape(heads, per_head, width)
    d_attn = lax.dot_general(
        w_heads, d_out, (((2,), (1,)), ((), ())), preferred_element_type=F
    ).astype(BF)
    d_attn = jnp.transpose(d_attn, (0, 2, 1))
    d_heads = lax.all_to_all(d_attn, SEQ, split_axis=0, concat_axis=0, tiled=True)

    places = [(0, 0), (1, 0), (0, -1), (0, 1), (0, 2), (1, -1), (1, 1), (1, 2)]
    order = jnp.stack(
        [(((yi + a) % 2) * 4 + (zi + b) % 4) * 2 + (ci + k) % 2 for k in (0, 1) for a, b in places]
    ).astype(jnp.int32)
    inner = jnp.arange(rows, dtype=jnp.int32)[None, :]
    valid = (inner < vrows) | (order[:, None] * trows + inner - vrows < prompt_len[0])
    bias = jnp.where(valid, 0.0, -1e30).astype(F).reshape(1, 2 * len(places) * rows)

    attn, d_qkv, gains = attention(
        order, own, sib, bias, d_heads, q_gain[None], k_gain[None]
    )
    n_own = len(places) * rows
    d_own = d_qkv[:n_own]
    d_sib = cc(d_qkv[n_own:])
    d_both = jnp.concatenate([d_own, d_sib], axis=1)

    def partial(place):
        piece = d_both[place * rows : (place + 1) * rows]
        return lax.dot_general(piece, w_both, (((1,), (1,)), ((), ())), preferred_element_type=F)

    def plus(base, got, start, stop):
        return base + jnp.pad(got.astype(F), ((start, rows - stop), (0, 0)))

    p_yc = partial(7).astype(BF)
    r_c = yy(p_yc[cut:])
    r_ya = zm(p_yc[:mid])
    r_yb = zp(p_yc[mid:cut])
    p_ya = plus(partial(5), r_ya, 0, mid).astype(BF)
    p_yb = plus(partial(6), r_yb, mid, cut).astype(BF)
    p_c = plus(partial(4), r_c, cut, rows).astype(BF)
    s_a = yy(p_ya[cut:])
    s_b = yy(p_yb[cut:])
    s_y1 = zm(p_ya[:cut])
    s_y2 = zp(p_yb[:cut])
    t_a = zm(p_c[:half])
    t_b = zp(p_c[half:])
    p_a = plus(plus(partial(2), s_a, cut, rows), t_a, 0, half).astype(BF)
    p_b = plus(plus(partial(3), s_b, cut, rows), t_b, half, rows).astype(BF)
    p_y = plus(partial(1), s_y1.astype(F) + s_y2.astype(F), 0, cut).astype(BF)
    d_h = partial(0) + (zm(p_a).astype(F) + zp(p_b).astype(F) + yy(p_y).astype(F))

    h_all = jnp.concatenate([h_one, h_two], axis=0)
    g_sib = lax.dot_general(h_all, d_sib, (((0,), (0,)), ((), ())), preferred_element_type=F)
    g_own = lax.dot_general(h_all, d_own, (((0,), (0,)), ((), ())), preferred_element_type=F)
    g_all = g_own + cc(g_sib.astype(BF)).astype(F)
    g_all = g_all.astype(BF).reshape(2, 4, width // 8, cols)
    xi = lax.axis_index("x")
    at = lambda r: lax.dynamic_index_in_dim(g_all, (xi + r) % 4, 1, keepdims=False)
    far = at(2)
    got_b = ring(far[0], "x", -1)
    got_a = ring(far[1], "x", 1)
    near_a, near_b = at(1), at(3)
    near_a = jnp.stack([near_a[0], near_a[1] + got_a])
    near_b = jnp.stack([near_b[0] + got_b, near_b[1]])
    mine = (
        at(0).astype(F) + ring(near_a, "x", 1).astype(F) + ring(near_b, "x", -1).astype(F)
    )
    hi = lax.axis_index("yh")
    keep = lax.dynamic_index_in_dim(mine, hi, 0, keepdims=False)
    give = lax.dynamic_index_in_dim(mine, 1 - hi, 0, keepdims=False).astype(BF)
    grad_w = (keep + ring(give, "yh", 1).astype(F)).reshape(width // 8, 3, per_head)

    attn_tok = lax.all_to_all(attn, SEQ, split_axis=0, concat_axis=0, tiled=True)
    out = lax.dot_general(
        attn_tok, w_heads, (((0, 2), (0, 1)), ((), ())), preferred_element_type=F
    )
    result = (joined + gate * out).astype(BF)

    t = d_h * (1.0 + scale)
    back = rstd * (
        t
        - jnp.mean(t, axis=-1, keepdims=True)
        - normed * jnp.mean(t * normed, axis=-1, keepdims=True)
    )
    d_joined = (dy + back).astype(BF)
    mod_local = jnp.stack(
        [jnp.sum(d_h, axis=0), jnp.sum(d_h * normed, axis=0), jnp.sum(dy * out, axis=0)], axis=0
    ).astype(BF)

    def total(values, axes):
        size = lax.axis_size(axes)
        wide = jnp.broadcast_to(values[None], (size,) + values.shape)
        return jnp.sum(
            lax.all_to_all(wide, axes, split_axis=0, concat_axis=0, tiled=True).astype(F), axis=0
        )

    grad_mod = total(mod_local, SEQ)
    grad_gain = total(gains, EVERY)
    return (
        result[None, :vrows],
        result[None, vrows:],
        d_joined[None, :vrows],
        d_joined[None, vrows:],
        grad_mod[None],
        grad_w,
        grad_gain,
    )


def solution(mesh):
    fine = Mesh(mesh.devices.reshape(2, 4, 2, 4, 2), EVERY)
    tokens = P(SECTION, SEQ, None)
    return jax.shard_map(
        per_device,
        mesh=fine,
        in_specs=(
            tokens,
            tokens,
            P(SECTION),
            P(SECTION, None, None),
            P(),
            P(),
            P(None, None, SEQ),
            P(),
            tokens,
            tokens,
        ),
        out_specs=(
            tokens,
            tokens,
            tokens,
            tokens,
            P(SECTION, None, None),
            P(SECTION, None, SEQ),
            P(),
        ),
        check_vma=False,
    )
```

```python
import functools
import jax
import jax.numpy as jnp
from jax import lax
from jax.experimental import pallas as pl
from jax.experimental.pallas import tpu as pltpu
from jax.sharding import Mesh
from jax.sharding import PartitionSpec as P

BF = jnp.bfloat16
F = jnp.float32
HD = 128
SEQ = ("y", "z", "core")
SECTION = ("yh", "x")
EVERY = SECTION + SEQ
NT = (((1,), (1,)), ((), ()))
TN = (((0,), (0,)), ((), ()))


def shape(dims, kind=BF):
    return jax.ShapeDtypeStruct(dims, kind)


def whole(dims):
    return pl.BlockSpec(dims, lambda *_: (0,) * len(dims))


def call(kernel, outs, mib=48, flops=0, moved=0, **more):
    return pl.pallas_call(
        kernel,
        out_shape=outs,
        compiler_params=pltpu.CompilerParams(vmem_limit_bytes=mib * 2**20),
        cost_estimate=pl.CostEstimate(flops=flops, bytes_accessed=moved, transcendentals=0),
        **more,
    )


def layer_norm(x):
    center = x - jnp.mean(x, axis=-1, keepdims=True)
    rstd = lax.rsqrt(jnp.mean(center * center, axis=-1, keepdims=True) + 1e-06)
    return center * rstd, rstd


def modulate_kernel(video_ref, text_ref, mod_ref, h_ref):
    shift, scale = mod_ref[0:1, :], 1.0 + mod_ref[1:2, :]
    vrows = video_ref.shape[0]
    for i in range(0, vrows, 16):
        normed, _ = layer_norm(video_ref[i : i + 16, :].astype(F))
        h_ref[i : i + 16, :] = (normed * scale + shift).astype(BF)
    normed, _ = layer_norm(text_ref[...].astype(F))
    h_ref[vrows:, :] = (normed * scale + shift).astype(BF)


def d_attn_kernel(video_ref, text_ref, gate_ref, w_ref, out_ref, d_out):
    @pl.when(pl.program_id(0) == 0)
    def _():
        vrows = video_ref.shape[0]
        d_out[0:vrows, :] = (video_ref[...].astype(F) * gate_ref[...]).astype(BF)
        d_out[vrows:, :] = (text_ref[...].astype(F) * gate_ref[...]).astype(BF)

    got = lax.dot_general(d_out[...], w_ref[...], NT, preferred_element_type=F)
    for j in range(out_ref.shape[0]):
        out_ref[j] = got[:, j * HD : (j + 1) * HD].astype(BF)


def out_kernel(attn_ref, w_ref, video_ref, text_ref, dv_ref, dt_ref, gate_ref, ov_ref, ot_ref, dg_ref, tok):
    rows = tok.shape[0]

    @pl.when(pl.program_id(0) == 0)
    def _():
        for j in range(attn_ref.shape[0]):
            tok[:, j * HD : (j + 1) * HD] = attn_ref[j, 0:rows, :]

    out = jnp.dot(tok[...], w_ref[...], preferred_element_type=F)
    vrows = video_ref.shape[0]
    top, low = out[:vrows], out[vrows:]
    gate = gate_ref[...]
    ov_ref[...] = (video_ref[...].astype(F) + gate * top).astype(BF)
    ot_ref[...] = (text_ref[...].astype(F) + gate * low).astype(BF)
    dg_ref[...] = jnp.sum(dv_ref[...].astype(F) * top, axis=0, keepdims=True) + jnp.sum(
        dt_ref[...].astype(F) * low, axis=0, keepdims=True
    )


def far_kernel(cut, mid, half, own_ref, sib_ref, w_ref, ym_ref, yp_ref, yy_ref, m1_ref, m2_ref, m3_ref):
    n = own_ref.shape[1]
    got = lax.dot_general(own_ref[...], w_ref[:, :n], NT, preferred_element_type=F)
    got += lax.dot_general(sib_ref[...], w_ref[:, n:], NT, preferred_element_type=F)
    rows = got.shape[0] // 4
    c, ya, yb, yc = (got[i * rows : (i + 1) * rows] for i in range(4))
    ym_ref[...] = yc[:mid].astype(BF)
    yp_ref[...] = yc[mid:cut].astype(BF)
    yy_ref[...] = yc[cut:].astype(BF)
    m1_ref[...] = jnp.concatenate([ya[:cut], c[:half]], axis=0).astype(BF)
    m2_ref[...] = jnp.concatenate([yb[:cut], c[half:]], axis=0).astype(BF)
    m3_ref[...] = jnp.concatenate([ya[cut:], yb[cut:]], axis=0).astype(BF)


def near_kernel(own_ref, sib_ref, w_ref, o_ref, y_ref, a_ref, b_ref):
    n = own_ref.shape[1]
    got = lax.dot_general(own_ref[...], w_ref[:, :n], NT, preferred_element_type=F)
    got += lax.dot_general(sib_ref[...], w_ref[:, n:], NT, preferred_element_type=F)
    rows = got.shape[0] // 4
    for i, ref in enumerate((o_ref, y_ref, a_ref, b_ref)):
        ref[...] = got[i * rows : (i + 1) * rows].astype(BF)


def grad_w_kernel(place_ref, h_ref, own_ref, sib_ref, own_out, sib_out):
    for d_ref, out in ((own_ref, own_out), (sib_ref, sib_out)):
        got = lax.dot_general(h_ref[...], d_ref[...], TN, preferred_element_type=F)
        for j in range(3):
            out[0, j] = got[:, j * HD : (j + 1) * HD].astype(BF)


def tail_kernel(o_ref, ra_ref, rb_ref, ry_ref, video_ref, text_ref, dv_ref, dt_ref, mod_ref, dg_ref, gv_ref, gt_ref, m_ref):
    scale = 1.0 + mod_ref[1:2, :]
    vrows = video_ref.shape[0]
    first = jnp.zeros((8, scale.shape[1]), F)
    second = first
    everything = lambda at, n: (
        o_ref[at : at + n, :].astype(F)
        + ra_ref[at : at + n, :].astype(F)
        + rb_ref[at : at + n, :].astype(F)
        + ry_ref[at : at + n, :].astype(F)
    )
    fold = lambda v: jnp.sum(v.reshape(v.shape[0] // 8, 8, v.shape[1]), axis=0)
    pieces = [(i, 16, video_ref, dv_ref, gv_ref, i) for i in range(0, vrows, 16)]
    pieces.append((vrows, text_ref.shape[0], text_ref, dt_ref, gt_ref, 0))
    for at, n, x_ref, dy_ref, g_ref, lo in pieces:
        d_h = everything(at, n)
        normed, rstd = layer_norm(x_ref[lo : lo + n, :].astype(F))
        t = d_h * scale
        back = rstd * (
            t
            - jnp.mean(t, axis=-1, keepdims=True)
            - normed * jnp.mean(t * normed, axis=-1, keepdims=True)
        )
        g_ref[lo : lo + n, :] = (dy_ref[lo : lo + n, :].astype(F) + back).astype(BF)
        first += fold(d_h)
        second += fold(d_h * normed)
    rows = [jnp.sum(v, axis=0, keepdims=True) for v in (first, second)] + [dg_ref[...]]
    m = jnp.concatenate(rows, axis=0).astype(BF)
    m_ref[...] = jnp.broadcast_to(m[None], m_ref.shape)


def rms(x):
    r = lax.rsqrt(jnp.mean(x * x, axis=-1, keepdims=True) + 1e-6)
    return x * r, r


def rms_back(t, xh, r):
    return r * (t - xh * jnp.mean(t * xh, axis=-1, keepdims=True))


def attn_kernel(
    rows, order_ref, q1_ref, q2_ref, s1_ref, s2_ref, bias_ref, do_ref, gq_ref, gk_ref,
    attn_ref, own_ref, give_ref, kn_s, v_s, dk_s, dv_s, gain_s,
):
    block = q1_ref.shape[0]
    parts = (q1_ref, q2_ref, s1_ref, s2_ref)
    outs = ((own_ref, 0), (own_ref, block), (give_ref, 0), (give_ref, block))
    per = block // rows
    scale = HD**-0.5
    step = pl.program_id(0)
    gq, gk = gq_ref[...], gk_ref[...]

    @pl.when(step == 0)
    def _():
        for i, ref in enumerate(parts):
            xh, _ = rms(ref[:, HD : 2 * HD].astype(F))
            kn_s[i * block : (i + 1) * block, :] = (xh * gk).astype(BF)
            v_s[i * block : (i + 1) * block, :] = ref[:, 2 * HD : 3 * HD]
        dk_s[...] = jnp.zeros_like(dk_s)
        dv_s[...] = jnp.zeros_like(dv_s)
        gain_s[...] = jnp.zeros_like(gain_s)

    def body(i):
        out, at = outs[i]
        xh, r = rms(parts[i][:, 0:HD].astype(F))
        qn = (xh * (gq * scale)).astype(BF)
        s = lax.dot_general(qn, kn_s[...], NT, preferred_element_type=F) + bias_ref[...]
        e = jnp.exp(s)
        linv = 1.0 / jnp.sum(e, axis=-1, keepdims=True)
        eb = e.astype(BF)
        o = jnp.dot(eb, v_s[...], preferred_element_type=F) * linv
        do = jnp.concatenate(
            [do_ref[order_ref[i * per + j]].astype(F) for j in range(per)], axis=0
        )
        for j in range(per):
            attn_ref[order_ref[i * per + j], 0:rows, :] = o[j * rows : (j + 1) * rows].astype(BF)
        dn = do * linv
        dnb = dn.astype(BF)
        delta = jnp.sum(dn * o, axis=-1, keepdims=True)
        dp = lax.dot_general(dnb, v_s[...], NT, preferred_element_type=F)
        ds = (e * (dp - delta)).astype(BF)
        dq = jnp.dot(ds, kn_s[...], preferred_element_type=F)
        dk_s[...] += lax.dot_general(ds, qn, TN, preferred_element_type=F)
        dv_s[...] += lax.dot_general(eb, dnb, TN, preferred_element_type=F)
        gain_s[0:1, :] += jnp.sum(dq * xh, axis=0, keepdims=True) * scale
        out[at : at + block, 0:HD] = rms_back(dq * (gq * scale), xh, r).astype(BF)

    for i in range(4):
        pl.when(step == i)(functools.partial(body, i))

    @pl.when(step == 3)
    def _():
        for i, ref in enumerate(parts):
            out, at = outs[i]
            xh, r = rms(ref[:, HD : 2 * HD].astype(F))
            dk = dk_s[i * block : (i + 1) * block, :]
            gain_s[1:2, :] += jnp.sum(dk * xh, axis=0, keepdims=True)
            out[at : at + block, HD : 2 * HD] = rms_back(dk * gk, xh, r).astype(BF)
            out[at : at + block, 2 * HD :] = dv_s[i * block : (i + 1) * block, :].astype(BF)
        gains = gain_s[...]
        high = gains.astype(BF).astype(F)
        low = (gains - high).astype(BF).astype(F)
        rest = gains - high - low
        tail = jnp.concatenate([high[0:2], low[0:2], rest[0:2], jnp.zeros((2, HD), F)], axis=0)
        attn_ref[:, rows:, :] = jnp.broadcast_to(tail.astype(BF)[None], (attn_ref.shape[0], 8, HD))


def ring(values, axis, distance):
    size = lax.axis_size(axis)
    return lax.ppermute(values, axis, [(i, (i + distance) % size) for i in range(size)])


def tie(values, *after):
    return lax.optimization_barrier((values, *after))[0]


def per_device(
    video, text, prompt_len, modulation, q_gain, k_gain, w_qkv, w_out, cot_video, cot_text
):
    video, text, cot_video, cot_text, modulation = (
        a[0] for a in (video, text, cot_video, cot_text, modulation)
    )
    vrows, trows = video.shape[0], text.shape[0]
    rows, width = vrows + trows, video.shape[1]
    heads = w_out.shape[0] // HD
    cols = 3 * HD
    yi, zi, ci = (lax.axis_index(a) for a in SEQ)
    zp = functools.partial(ring, axis="z", distance=1)
    zm = functools.partial(ring, axis="z", distance=-1)
    yy = functools.partial(ring, axis="y", distance=1)
    cc = functools.partial(ring, axis="core", distance=1)
    gate = modulation[2:3]
    cut, mid, half = 80, 40, 72

    h = call(modulate_kernel, shape((rows, width)))(video, text, modulation)
    h_y, h_a, h_b = yy(h), zp(h), zm(h)

    w_own = w_qkv.reshape(width, cols)
    w_both = jnp.concatenate([w_own, cc(w_own)], axis=1)
    step = 2 * HD
    d_attn = call(
        d_attn_kernel,
        shape((heads, rows, HD)),
        flops=2 * rows * width * heads * HD,
        moved=2 * heads * HD * width,
        grid=(heads * HD // step,),
        in_specs=[
            whole((vrows, width)),
            whole((trows, width)),
            whole((1, width)),
            pl.BlockSpec((step, width), lambda i: (i, 0)),
        ],
        out_specs=pl.BlockSpec((step // HD, rows, HD), lambda i: (i, 0, 0)),
        scratch_shapes=[pltpu.VMEM((rows, width), BF)],
    )(cot_video, cot_text, gate, w_out)

    h_c = jnp.concatenate([zp(h_a[:half]), zm(h_b[half:])], axis=0)
    d_a, d_b = zp(h_y[:cut]), zm(h_y[:cut])
    e_a, e_b = yy(h_a[cut:]), yy(h_b[cut:])
    d_heads = lax.all_to_all(
        tie(d_attn, h_y, h_a, h_b), SEQ, split_axis=0, concat_axis=0, tiled=True
    )
    h_one = jnp.concatenate([h, h_y, h_a, h_b], axis=0)
    qkv_one = jnp.dot(h_one, w_both, preferred_element_type=F).astype(BF)
    sib_one = cc(qkv_one[:, cols:])
    f_a, f_b, f_c = zp(d_a[:mid]), zm(d_b[mid:]), yy(tie(h_c[cut:], qkv_one, d_heads))
    h_two = jnp.concatenate([h_c, d_a, e_a, d_b, e_b, f_a, f_b, f_c], axis=0)
    qkv_two = jnp.dot(h_two, w_both, preferred_element_type=F).astype(BF)
    sib_two = cc(qkv_two[:, cols:])

    places = [(0, 0), (1, 0), (0, -1), (0, 1), (0, 2), (1, -1), (1, 1), (1, 2)]
    order = jnp.stack(
        [(((yi + a) % 2) * 4 + (zi + b) % 4) * 2 + (ci + k) % 2 for k in (0, 1) for a, b in places]
    ).astype(jnp.int32)
    inner = jnp.arange(rows, dtype=jnp.int32)[None, :]
    valid = (inner < vrows) | (order[:, None] * trows + inner - vrows < prompt_len[0])
    bias = jnp.where(valid, 0.0, -1e30).astype(F).reshape(1, 2 * len(places) * rows)

    n = len(places) * rows
    block = n // 2
    attn, d_own, d_give = call(
        functools.partial(attn_kernel, rows),
        (shape((heads, rows + 8, HD)), shape((n, cols)), shape((n, cols))),
        mib=56,
        flops=12 * (2 * n) ** 2 * HD,
        moved=n * HD * 24,
        grid_spec=pltpu.PrefetchScalarGridSpec(
            num_scalar_prefetch=1,
            grid=(4,),
            in_specs=[whole(a) for a in ((block, 2 * cols),) * 2 + ((block, cols),) * 2]
            + [whole((1, 2 * n)), whole((heads, rows, HD)), whole((1, HD)), whole((1, HD))],
            out_specs=[whole((heads, rows + 8, HD)), whole((n, cols)), whole((n, cols))],
            scratch_shapes=[
                pltpu.VMEM((2 * n, HD), BF),
                pltpu.VMEM((2 * n, HD), BF),
                pltpu.VMEM((2 * n, HD), F),
                pltpu.VMEM((2 * n, HD), F),
                pltpu.VMEM((8, HD), F),
            ],
        ),
    )(order, qkv_one, qkv_two, sib_one, sib_two, bias, d_heads, q_gain[None], k_gain[None])

    d_sib = cc(d_give)
    attn_tok = lax.all_to_all(attn, SEQ, split_axis=0, concat_axis=0, tiled=True)

    strip = 512
    strips = lambda count: pl.BlockSpec((count, strip), lambda i: (0, i))
    sizes = (mid, cut - mid, rows - cut, cut + half, cut + rows - half, 2 * (rows - cut))
    half_specs = lambda at: [
        pl.BlockSpec((block, cols), lambda i: (at, 0)),
        pl.BlockSpec((block, cols), lambda i: (at, 0)),
        pl.BlockSpec((strip, 2 * cols), lambda i: (i, 0)),
    ]
    work = dict(flops=4 * block * width * cols, moved=4 * width * cols, grid=(width // strip,))
    y_m, y_p, y_y, m_1, m_2, m_3 = call(
        functools.partial(far_kernel, cut, mid, half),
        tuple(shape((k, width)) for k in sizes),
        in_specs=half_specs(1),
        out_specs=[strips(k) for k in sizes],
        **work,
    )(d_own, d_sib, w_both)
    r_ya, r_yb, r_c = zm(y_m), zp(y_p), yy(y_y)
    p_o, p_y, p_a, p_b = call(
        near_kernel,
        (shape((rows, width)),) * 4,
        in_specs=half_specs(0),
        out_specs=[strips(rows)] * 4,
        **work,
    )(d_own, d_sib, w_both)

    def plus(base, *parts):
        total = base.astype(F)
        for got, at in parts:
            total = total + jnp.pad(
                got.astype(F), ((at, base.shape[0] - at - got.shape[0]), (0, 0))
            )
        return total.astype(BF)

    got_1 = zm(plus(m_1, (r_ya, 0)))
    got_2 = zp(plus(m_2, (r_yb, mid), (r_c, 2 * cut - half)))
    got_3 = yy(m_3)
    part = rows - cut
    p_y = plus(p_y, (got_1[:cut], 0), (got_2[:cut], 0))
    p_a = plus(p_a, (got_1[cut:], 0), (got_3[:part], cut))
    p_b = plus(p_b, (got_2[cut:], half), (got_3[part:], cut))
    last_a, last_b, last_y = zm(p_a), zp(p_b), yy(p_y)

    xi, hi = lax.axis_index("x"), lax.axis_index("yh")
    h_all = jnp.concatenate([h_one, h_two], axis=0)
    wide = width // 8
    place = lambda i, p: (((i % 4 - p[0]) % 4) * 2 + (i // 4 - p[1]) % 2, 0, 0, 0)
    g_own, g_sib = call(
        grad_w_kernel,
        (shape((8, 3, wide, HD)),) * 2,
        flops=4 * n * width * cols,
        moved=4 * n * width,
        grid_spec=pltpu.PrefetchScalarGridSpec(
            num_scalar_prefetch=1,
            grid=(8,),
            in_specs=[
                pl.BlockSpec((n, wide), lambda i, p: (0, i)),
                whole((n, cols)),
                whole((n, cols)),
            ],
            out_specs=[pl.BlockSpec((1, 3, wide, HD), place)] * 2,
        ),
    )(jnp.stack([xi - 4, hi - 2]).astype(jnp.int32), h_all, d_own, d_sib)
    g_got = cc(g_sib)
    total = lambda i: g_own[i].astype(F) + g_got[i].astype(F)
    near = lambda r: (total(2 * r), total(2 * r + 1))
    far_0, far_1 = near(2)
    got_b = ring(far_0.astype(BF), "x", -1)
    got_a = ring(far_1.astype(BF), "x", 1)
    a_0, a_1 = near(1)
    b_0, b_1 = near(3)
    send_a = jnp.stack([a_0, a_1 + got_a.astype(F)]).astype(BF)
    send_b = jnp.stack([b_0 + got_b.astype(F), b_1]).astype(BF)
    back_a, back_b = ring(send_a, "x", 1), ring(send_b, "x", -1)
    keep, give = near(0)
    give = give + back_a[1].astype(F) + back_b[1].astype(F)
    keep = keep + back_a[0].astype(F) + back_b[0].astype(F)
    grad_w = keep + ring(give.astype(BF), "yh", 1).astype(F)
    grad_w = jnp.transpose(grad_w, (1, 0, 2))

    gains = jnp.sum(attn_tok[:, rows:, :].astype(F), axis=0)
    gains = gains[0:2] + gains[2:4] + gains[4:6]
    gains = gains + ring(gains, "x", 2)
    gains = gains + ring(gains, "x", 1)
    grad_gain = gains + ring(gains, "yh", 1)

    out_video, out_text, d_gate = call(
        out_kernel,
        (shape((vrows, width)), shape((trows, width)), shape((1, width), F)),
        flops=2 * rows * width * heads * HD,
        moved=2 * heads * HD * width,
        grid=(width // strip,),
        in_specs=[
            whole((heads, rows + 8, HD)),
            pl.BlockSpec((heads * HD, strip), lambda i: (0, i)),
        ]
        + [strips(k) for k in (vrows, trows, vrows, trows, 1)],
        out_specs=[strips(k) for k in (vrows, trows, 1)],
        scratch_shapes=[pltpu.VMEM((rows, heads * HD), BF)],
    )(attn_tok, w_out, video, text, cot_video, cot_text, gate)

    grad_video, grad_text, wide_mod = call(
        tail_kernel,
        (shape((vrows, width)), shape((trows, width)), shape((heads, 3, width))),
    )(p_o, last_a, last_b, last_y, video, text, cot_video, cot_text, modulation, d_gate)
    grad_mod = jnp.sum(
        lax.all_to_all(wide_mod, SEQ, split_axis=0, concat_axis=0, tiled=True).astype(F), axis=0
    )
    return (
        out_video[None],
        out_text[None],
        grad_video[None],
        grad_text[None],
        grad_mod[None],
        grad_w,
        grad_gain,
    )


def solution(mesh):
    fine = Mesh(mesh.devices.reshape(2, 4, 2, 4, 2), EVERY)
    tokens = P(SECTION, SEQ, None)
    sample = P(SECTION, None, None)
    return jax.shard_map(
        per_device,
        mesh=fine,
        in_specs=(tokens, tokens, P(SECTION), sample, P(), P(), P(None, None, SEQ), P(), tokens, tokens),
        out_specs=(tokens, tokens, tokens, tokens, sample, P(SECTION, None, SEQ), P()),
        check_vma=False,
    )
```

```python
import functools
import jax
import jax.numpy as jnp
from jax import lax
from jax.experimental import pallas as pl
from jax.experimental.pallas import tpu as pltpu
from jax.sharding import Mesh
from jax.sharding import PartitionSpec as P

BF = jnp.bfloat16
F = jnp.float32
HD = 128
SEQ = ("y", "z", "core")
SECTION = ("yh", "x")
EVERY = SECTION + SEQ
NT = (((1,), (1,)), ((), ()))
TN = (((0,), (0,)), ((), ()))
PLACES = [(0, 0), (1, 0), (0, -1), (0, 1), (0, 2), (1, -1), (1, 1), (1, 2)]


def shape(dims, kind=BF):
    return jax.ShapeDtypeStruct(dims, kind)


def whole(dims):
    return pl.BlockSpec(dims, lambda *_: (0,) * len(dims))


def call(kernel, outs, mib=48, us=0, **more):
    return pl.pallas_call(
        kernel,
        out_shape=outs,
        compiler_params=pltpu.CompilerParams(vmem_limit_bytes=mib * 2**20),
        cost_estimate=pl.CostEstimate(flops=int(us * 1.1e9) + 1, bytes_accessed=1, transcendentals=0),
        **more,
    )


def side_by_side(*refs):
    return jnp.concatenate([ref[j] for ref in refs for j in range(3)], axis=1)


def layer_norm(x):
    center = x - jnp.mean(x, axis=-1, keepdims=True)
    rstd = lax.rsqrt(jnp.mean(center * center, axis=-1, keepdims=True) + 1e-06)
    return center * rstd, rstd


def modulate_kernel(video_ref, text_ref, mod_ref, h_ref, top_ref, low_ref):
    shift, scale = mod_ref[0:1, :], 1.0 + mod_ref[1:2, :]
    vrows, cut = video_ref.shape[0], top_ref.shape[0]
    for i in range(0, vrows, 16):
        normed, _ = layer_norm(video_ref[i : i + 16, :].astype(F))
        ref, at = (top_ref, i) if i < cut else (low_ref, i - cut)
        h = (normed * scale + shift).astype(BF)
        ref[at : at + 16, :] = h
        h_ref[i : i + 16, :] = h
    normed, _ = layer_norm(text_ref[...].astype(F))
    h = (normed * scale + shift).astype(BF)
    low_ref[vrows - cut :, :] = h
    h_ref[vrows:, :] = h


def qkv_kernel(pieces, *refs):
    own_w, sib_w = refs[pieces : pieces + 2]
    h_ref, own_ref, sib_ref, acc = refs[pieces + 2 :]
    h = jnp.concatenate([ref[...] for ref in refs[:pieces]], axis=0)
    h_ref[...] = h
    w = side_by_side(own_w, sib_w)
    got = jnp.dot(h, w, preferred_element_type=F)
    step = pl.program_id(0)

    @pl.when(step == 0)
    def _():
        acc[...] = got

    @pl.when(step > 0)
    def _():
        acc[...] += got

    @pl.when(step == pl.num_programs(0) - 1)
    def _():
        cols = own_ref.shape[1]
        own_ref[...] = acc[:, :cols].astype(BF)
        sib_ref[...] = acc[:, cols:].astype(BF)


def d_attn_kernel(video_ref, text_ref, gate_ref, w_ref, out_ref, d_out):
    @pl.when(pl.program_id(0) == 0)
    def _():
        vrows = video_ref.shape[0]
        d_out[0:vrows, :] = (video_ref[...].astype(F) * gate_ref[...]).astype(BF)
        d_out[vrows:, :] = (text_ref[...].astype(F) * gate_ref[...]).astype(BF)

    got = lax.dot_general(d_out[...], w_ref[...], NT, preferred_element_type=F)
    for j in range(out_ref.shape[0]):
        out_ref[j] = got[:, j * HD : (j + 1) * HD].astype(BF)


def out_kernel(attn_ref, w_ref, video_ref, text_ref, dv_ref, dt_ref, gate_ref, ov_ref, ot_ref, dg_ref, tok):
    rows = tok.shape[0]

    @pl.when(pl.program_id(0) == 0)
    def _():
        for j in range(attn_ref.shape[0]):
            tok[:, j * HD : (j + 1) * HD] = attn_ref[j, 0:rows, :]

    out = jnp.dot(tok[...], w_ref[...], preferred_element_type=F)
    vrows = video_ref.shape[0]
    top, low = out[:vrows], out[vrows:]
    gate = gate_ref[...]
    ov_ref[...] = (video_ref[...].astype(F) + gate * top).astype(BF)
    ot_ref[...] = (text_ref[...].astype(F) + gate * low).astype(BF)
    dg_ref[...] = jnp.sum(dv_ref[...].astype(F) * top, axis=0, keepdims=True) + jnp.sum(
        dt_ref[...].astype(F) * low, axis=0, keepdims=True
    )


def far_kernel(cut, own_ref, sib_ref, wo_ref, ws_ref, yct_ref, ycl_ref, ct_ref, cl_ref, yat_ref, ybl_ref, m_ref):
    d = jnp.concatenate([own_ref[...], sib_ref[...]], axis=1)
    w = side_by_side(wo_ref, ws_ref)
    got = lax.dot_general(d, w, NT, preferred_element_type=F)
    rows = got.shape[0] // 4
    c, ya, yb, yc = (got[i * rows : (i + 1) * rows] for i in range(4))
    yct_ref[...] = yc[:cut].astype(BF)
    ycl_ref[...] = yc[cut:].astype(BF)
    ct_ref[...] = c[:cut].astype(BF)
    cl_ref[...] = c[cut:].astype(BF)
    yat_ref[...] = ya[:cut].astype(BF)
    ybl_ref[...] = yb[cut:].astype(BF)
    m_ref[...] = jnp.concatenate([ya[cut:], yb[:cut]], axis=0).astype(BF)


def near_kernel(own_ref, sib_ref, wo_ref, ws_ref, o_ref, y_ref, a_ref, b_ref):
    d = jnp.concatenate([own_ref[...], sib_ref[...]], axis=1)
    w = side_by_side(wo_ref, ws_ref)
    got = lax.dot_general(d, w, NT, preferred_element_type=F)
    rows = got.shape[0] // 4
    for i, ref in enumerate((o_ref, y_ref, a_ref, b_ref)):
        ref[...] = got[i * rows : (i + 1) * rows].astype(BF)


def grad_w_kernel(place_ref, one_ref, two_ref, d_ref, out):
    h = jnp.concatenate([one_ref[...], two_ref[...]], axis=0)
    got = lax.dot_general(h, d_ref[...], TN, preferred_element_type=F)
    wide = out.shape[3]
    for i in range(4):
        at = (i - place_ref[0]) % 4
        for j in range(3):
            out[at, 0, j] = got[i * wide : (i + 1) * wide, j * HD : (j + 1) * HD].astype(BF)


def tail_kernel(o_ref, ra_ref, rb_ref, ry_ref, video_ref, text_ref, dv_ref, dt_ref, mod_ref, dg_ref, gv_ref, gt_ref, m_ref):
    scale = 1.0 + mod_ref[1:2, :]
    vrows = video_ref.shape[0]
    first = jnp.zeros((8, scale.shape[1]), F)
    second = first
    everything = lambda at, n: (
        o_ref[at : at + n, :].astype(F)
        + ra_ref[at : at + n, :].astype(F)
        + rb_ref[at : at + n, :].astype(F)
        + ry_ref[at : at + n, :].astype(F)
    )
    fold = lambda v: jnp.sum(v.reshape(v.shape[0] // 8, 8, v.shape[1]), axis=0)
    pieces = [(i, 16, video_ref, dv_ref, gv_ref, i) for i in range(0, vrows, 16)]
    pieces.append((vrows, text_ref.shape[0], text_ref, dt_ref, gt_ref, 0))
    for at, n, x_ref, dy_ref, g_ref, lo in pieces:
        d_h = everything(at, n)
        normed, rstd = layer_norm(x_ref[lo : lo + n, :].astype(F))
        t = d_h * scale
        back = rstd * (
            t
            - jnp.mean(t, axis=-1, keepdims=True)
            - normed * jnp.mean(t * normed, axis=-1, keepdims=True)
        )
        g_ref[lo : lo + n, :] = (dy_ref[lo : lo + n, :].astype(F) + back).astype(BF)
        first += fold(d_h)
        second += fold(d_h * normed)
    rows = [jnp.sum(v, axis=0, keepdims=True) for v in (first, second)] + [dg_ref[...]]
    m = jnp.concatenate(rows, axis=0).astype(BF)
    m_ref[...] = jnp.broadcast_to(m[None], m_ref.shape)


def rms(x):
    r = lax.rsqrt(jnp.mean(x * x, axis=-1, keepdims=True) + 1e-6)
    return x * r, r


def rms_back(t, xh, r):
    return r * (t - xh * jnp.mean(t * xh, axis=-1, keepdims=True))


def attn_kernel(
    rows, order_ref, q1_ref, q2_ref, s1_ref, s2_ref, bias_ref, do_ref, gq_ref, gk_ref,
    attn_ref, own_ref, give_ref, kn_s, v_s, dk_s, dv_s, gain_s,
):
    block = q1_ref.shape[0]
    parts = (q1_ref, q2_ref, s1_ref, s2_ref)
    outs = ((own_ref, 0), (own_ref, block), (give_ref, 0), (give_ref, block))
    per = block // rows
    scale = HD**-0.5
    step = pl.program_id(0)
    gq, gk = gq_ref[...], gk_ref[...]

    @pl.when(step == 0)
    def _():
        for i, ref in enumerate(parts):
            xh, _ = rms(ref[:, HD : 2 * HD].astype(F))
            kn_s[i * block : (i + 1) * block, :] = (xh * gk).astype(BF)
            v_s[i * block : (i + 1) * block, :] = ref[:, 2 * HD : 3 * HD]
        dk_s[...] = jnp.zeros_like(dk_s)
        dv_s[...] = jnp.zeros_like(dv_s)
        gain_s[...] = jnp.zeros_like(gain_s)

    def body(i):
        out, at = outs[i]
        xh, r = rms(parts[i][:, 0:HD].astype(F))
        qn = (xh * (gq * scale)).astype(BF)
        s = lax.dot_general(qn, kn_s[...], NT, preferred_element_type=F) + bias_ref[...]
        e = jnp.exp(s)
        linv = 1.0 / jnp.sum(e, axis=-1, keepdims=True)
        eb = e.astype(BF)
        o = jnp.dot(eb, v_s[...], preferred_element_type=F) * linv
        do = jnp.concatenate(
            [do_ref[order_ref[i * per + j]].astype(F) for j in range(per)], axis=0
        )
        for j in range(per):
            attn_ref[order_ref[i * per + j], 0:rows, :] = o[j * rows : (j + 1) * rows].astype(BF)
        dn = do * linv
        dnb = dn.astype(BF)
        delta = jnp.sum(dn * o, axis=-1, keepdims=True)
        dp = lax.dot_general(dnb, v_s[...], NT, preferred_element_type=F)
        ds = (e * (dp - delta)).astype(BF)
        dq = jnp.dot(ds, kn_s[...], preferred_element_type=F)
        dk_s[...] += lax.dot_general(ds, qn, TN, preferred_element_type=F)
        dv_s[...] += lax.dot_general(eb, dnb, TN, preferred_element_type=F)
        gain_s[0:1, :] += jnp.sum(dq * xh, axis=0, keepdims=True) * scale
        out[at : at + block, 0:HD] = rms_back(dq * (gq * scale), xh, r).astype(BF)

    for i in range(4):
        pl.when(step == i)(functools.partial(body, i))

    @pl.when(step == 3)
    def _():
        for i, ref in enumerate(parts):
            out, at = outs[i]
            xh, r = rms(ref[:, HD : 2 * HD].astype(F))
            dk = dk_s[i * block : (i + 1) * block, :]
            gain_s[1:2, :] += jnp.sum(dk * xh, axis=0, keepdims=True)
            out[at : at + block, HD : 2 * HD] = rms_back(dk * gk, xh, r).astype(BF)
            out[at : at + block, 2 * HD :] = dv_s[i * block : (i + 1) * block, :].astype(BF)
        gains = gain_s[...]
        high = gains.astype(BF).astype(F)
        low = (gains - high).astype(BF).astype(F)
        rest = gains - high - low
        tail = jnp.concatenate([high[0:2], low[0:2], rest[0:2], jnp.zeros((2, HD), F)], axis=0)
        attn_ref[:, rows:, :] = jnp.broadcast_to(tail.astype(BF)[None], (attn_ref.shape[0], 8, HD))


def ring(values, axis, distance):
    size = lax.axis_size(axis)
    return lax.ppermute(values, axis, [(i, (i + distance) % size) for i in range(size)])


def tie(values, *after):
    return lax.optimization_barrier((values, *after))[0]


def per_device(
    video, text, prompt_len, modulation, q_gain, k_gain, w_qkv, w_out, cot_video, cot_text
):
    video, text, cot_video, cot_text, modulation = (
        a[0] for a in (video, text, cot_video, cot_text, modulation)
    )
    vrows, trows = video.shape[0], text.shape[0]
    rows, width = vrows + trows, video.shape[1]
    heads = w_out.shape[0] // HD
    cols = 3 * HD
    yi, zi, ci = (lax.axis_index(a) for a in SEQ)
    zp = functools.partial(ring, axis="z", distance=1)
    zm = functools.partial(ring, axis="z", distance=-1)
    yy = functools.partial(ring, axis="y", distance=1)
    cc = functools.partial(ring, axis="core", distance=1)
    gate = modulation[2:3]
    cut = 64
    part = rows - cut

    h, h_t, h_l = call(
        modulate_kernel, (shape((rows, width)), shape((cut, width)), shape((part, width)))
    )(video, text, modulation)
    w_own = jnp.transpose(w_qkv, (1, 0, 2))
    step = 2 * HD
    per = 4

    w_sib = cc(w_own)
    a_t, b_l, y = zp(h_t), zm(h_l), yy(h)
    a_l, b_t = zp(h_l), zm(h_t)
    d_attn = call(
        d_attn_kernel,
        shape((heads, rows, HD)),
        us=10,
        grid=(2 * per,),
        in_specs=[
            whole((vrows, width)),
            whole((trows, width)),
            whole((1, width)),
            pl.BlockSpec((step, width), lambda i: (i, 0)),
        ],
        out_specs=pl.BlockSpec((step // HD, rows, HD), lambda i: (i, 0, 0)),
        scratch_shapes=[pltpu.VMEM((rows, width), BF)],
    )(cot_video, cot_text, tie(gate, h, w_sib), w_out)
    d_heads = lax.all_to_all(d_attn, SEQ, split_axis=0, concat_axis=0, tiled=True)
    ya_t, yb_l = zp(y[:cut]), zm(y[cut:])
    c_t, c_l = zp(a_t), zm(b_l)
    ya_l, yb_t = yy(a_l), yy(b_t)
    yc_t, yc_l = zp(ya_t), zm(yb_l)
    n = len(PLACES) * rows
    block = n // 2
    strip = 1024

    def project(us, *parts):
        return call(
            functools.partial(qkv_kernel, len(parts)),
            (shape((block, width)), shape((block, cols)), shape((block, cols))),
            mib=56,
            us=us,
            grid=(width // strip,),
            in_specs=[pl.BlockSpec((k.shape[0], strip), lambda i: (0, i)) for k in parts]
            + [pl.BlockSpec((3, strip, HD), lambda i: (0, i, 0))] * 2,
            out_specs=[
                pl.BlockSpec((block, strip), lambda i: (0, i)),
                whole((block, cols)),
                whole((block, cols)),
            ],
            scratch_shapes=[pltpu.VMEM((block, 2 * cols), F)],
        )(*parts, w_own, w_sib)

    h_one, own_one, sib_one = project(8, h, y, a_t, a_l, b_t, b_l)
    h_two, own_two, sib_two = project(0, c_t, c_l, ya_t, ya_l, yb_t, yb_l, yc_t, yc_l)
    sib_two = cc(sib_two)
    sib_one = cc(tie(sib_one, own_two))

    order = jnp.stack(
        [(((yi + a) % 2) * 4 + (zi + b) % 4) * 2 + (ci + k) % 2 for k in (0, 1) for a, b in PLACES]
    ).astype(jnp.int32)
    inner = jnp.arange(rows, dtype=jnp.int32)[None, :]
    valid = (inner < vrows) | (order[:, None] * trows + inner - vrows < prompt_len[0])
    bias = jnp.where(valid, 0.0, -1e30).astype(F).reshape(1, 2 * n)

    attn, d_own, d_give = call(
        functools.partial(attn_kernel, rows),
        (shape((heads, rows + 8, HD)), shape((n, cols)), shape((n, cols))),
        mib=56,
        grid_spec=pltpu.PrefetchScalarGridSpec(
            num_scalar_prefetch=1,
            grid=(4,),
            in_specs=[whole(a) for a in ((block, cols),) * 4]
            + [whole((1, 2 * n)), whole((heads, rows, HD)), whole((1, HD)), whole((1, HD))],
            out_specs=[whole((heads, rows + 8, HD)), whole((n, cols)), whole((n, cols))],
            scratch_shapes=[
                pltpu.VMEM((2 * n, HD), BF),
                pltpu.VMEM((2 * n, HD), BF),
                pltpu.VMEM((2 * n, HD), F),
                pltpu.VMEM((2 * n, HD), F),
                pltpu.VMEM((8, HD), F),
            ],
        ),
    )(order, own_one, own_two, sib_one, sib_two, bias, d_heads, q_gain[None], k_gain[None])

    d_sib = cc(d_give)

    xi, hi = lax.axis_index("x"), lax.axis_index("yh")
    wide = width // 8
    here = jnp.stack([xi - 4, hi - 2]).astype(jnp.int32)

    def weight_grad(here, d):
        return call(
            grad_w_kernel,
            shape((4, 2, 3, wide, HD)),
            grid_spec=pltpu.PrefetchScalarGridSpec(
                num_scalar_prefetch=1,
                grid=(2,),
                in_specs=[
                    pl.BlockSpec((block, 4 * wide), lambda i, p: (0, i)),
                    pl.BlockSpec((block, 4 * wide), lambda i, p: (0, i)),
                    whole((n, cols)),
                ],
                out_specs=pl.BlockSpec(
                    (4, 1, 3, wide, HD), lambda i, p: (0, (i - p[1]) % 2, 0, 0, 0)
                ),
            ),
        )(here, h_one, h_two, d)

    g_own = weight_grad(here, d_own)

    strips = lambda count: pl.BlockSpec((count, strip), lambda i: (0, i))
    sizes = (cut, part, cut, part, cut, part, rows)
    half_specs = lambda at: [
        pl.BlockSpec((block, cols), lambda i: (at, 0)),
        pl.BlockSpec((block, cols), lambda i: (at, 0)),
        pl.BlockSpec((3, strip, HD), lambda i: (0, i, 0)),
        pl.BlockSpec((3, strip, HD), lambda i: (0, i, 0)),
    ]
    work = dict(grid=(width // strip,), mib=56)
    yc_t, yc_l, c_t, c_l, ya_t, yb_l, m_y = call(
        functools.partial(far_kernel, cut),
        tuple(shape((k, width)) for k in sizes),
        in_specs=half_specs(1),
        out_specs=[strips(k) for k in sizes],
        **work,
    )(tie(d_own, g_own), d_sib, w_own, w_sib)
    r_ya, r_yb, got_m = zm(yc_t), zp(yc_l), yy(m_y)
    r_a, r_b = zm(c_t), zp(c_l)
    ya_t = (ya_t.astype(F) + r_ya.astype(F)).astype(BF)
    yb_l = (yb_l.astype(F) + r_yb.astype(F)).astype(BF)
    r_yt, r_yl = zm(ya_t), zp(yb_l)
    g_sib = weight_grad(tie(here, m_y), d_sib)
    attn_tok = lax.all_to_all(
        tie(attn, r_ya, r_yb), SEQ, split_axis=0, concat_axis=0, tiled=True
    )
    p_o, p_y, p_a, p_b = call(
        near_kernel,
        (shape((rows, width)),) * 4,
        in_specs=half_specs(0),
        out_specs=[strips(rows)] * 4,
        **work,
    )(tie(d_own, g_sib), d_sib, w_own, w_sib)

    def plus(base, top, low):
        return (base.astype(F) + jnp.concatenate([top, low], axis=0).astype(F)).astype(BF)

    p_a = plus(p_a, r_a, got_m[:part])
    p_b = plus(p_b, got_m[part:], r_b)
    p_y = plus(p_y, r_yt, r_yl)
    last_a, last_b, last_y = zm(p_a), zp(p_b), yy(p_y)

    g_got = cc(g_sib)
    total = lambda i: g_own[i // 2, i % 2].astype(F) + g_got[i // 2, i % 2].astype(F)
    near = lambda r: (total(2 * r), total(2 * r + 1))
    far_0, far_1 = near(2)
    got_b = ring(far_0.astype(BF), "x", -1)
    got_a = ring(far_1.astype(BF), "x", 1)
    a_0, a_1 = near(1)
    b_0, b_1 = near(3)
    send_a = jnp.stack([a_0, a_1 + got_a.astype(F)]).astype(BF)
    send_b = jnp.stack([b_0 + got_b.astype(F), b_1]).astype(BF)
    back_a, back_b = ring(send_a, "x", 1), ring(send_b, "x", -1)
    keep, give = near(0)
    give = give + back_a[1].astype(F) + back_b[1].astype(F)
    keep = keep + back_a[0].astype(F) + back_b[0].astype(F)
    grad_w = keep + ring(give.astype(BF), "yh", 1).astype(F)
    grad_w = jnp.transpose(grad_w, (1, 0, 2))

    gains = jnp.sum(attn_tok[:, rows:, :].astype(F), axis=0)
    gains = gains[0:2] + gains[2:4] + gains[4:6]
    gains = gains + ring(gains, "x", 2)
    gains = gains + ring(gains, "x", 1)
    grad_gain = gains + ring(gains, "yh", 1)

    out_video, out_text, d_gate = call(
        out_kernel,
        (shape((vrows, width)), shape((trows, width)), shape((1, width), F)),
        grid=(width // strip,),
        mib=56,
        in_specs=[
            whole((heads, rows + 8, HD)),
            pl.BlockSpec((heads * HD, strip), lambda i: (0, i)),
        ]
        + [strips(k) for k in (vrows, trows, vrows, trows, 1)],
        out_specs=[strips(k) for k in (vrows, trows, 1)],
        scratch_shapes=[pltpu.VMEM((rows, heads * HD), BF)],
    )(tie(attn_tok, p_o, far_0), w_out, video, text, cot_video, cot_text, gate)

    grad_video, grad_text, wide_mod = call(
        tail_kernel,
        (shape((vrows, width)), shape((trows, width)), shape((heads, 3, width))),
    )(p_o, last_a, last_b, last_y, video, text, cot_video, cot_text, modulation, d_gate)
    grad_mod = jnp.sum(
        lax.all_to_all(wide_mod, SEQ, split_axis=0, concat_axis=0, tiled=True).astype(F), axis=0
    )
    return (
        out_video[None],
        out_text[None],
        grad_video[None],
        grad_text[None],
        grad_mod[None],
        grad_w,
        grad_gain,
    )


def solution(mesh):
    fine = Mesh(mesh.devices.reshape(2, 4, 2, 4, 2), EVERY)
    tokens = P(SECTION, SEQ, None)
    sample = P(SECTION, None, None)
    return jax.shard_map(
        per_device,
        mesh=fine,
        in_specs=(tokens, tokens, P(SECTION), sample, P(), P(), P(None, None, SEQ), P(), tokens, tokens),
        out_specs=(tokens, tokens, tokens, tokens, sample, P(SECTION, None, SEQ), P()),
        check_vma=False,
    )
```

```python
import functools
import jax
import jax.numpy as jnp
from jax import lax
from jax.experimental import pallas as pl
from jax.experimental.pallas import tpu as pltpu
from jax.sharding import Mesh
from jax.sharding import PartitionSpec as P

BF = jnp.bfloat16
F = jnp.float32
HD = 128
SEQ = ("y", "z", "core")
SECTION = ("yh", "x")
EVERY = SECTION + SEQ
NT = (((1,), (1,)), ((), ()))
TN = (((0,), (0,)), ((), ()))
PLACES = [(0, 0), (1, 0), (0, -1), (0, 1), (0, 2), (1, -1), (1, 1), (1, 2)]


def shape(dims, kind=BF):
    return jax.ShapeDtypeStruct(dims, kind)


def whole(dims):
    return pl.BlockSpec(dims, lambda *_: (0,) * len(dims))


def call(kernel, outs, mib=48, us=0, **more):
    return pl.pallas_call(
        kernel,
        out_shape=outs,
        compiler_params=pltpu.CompilerParams(vmem_limit_bytes=mib * 2**20),
        cost_estimate=pl.CostEstimate(flops=int(us * 1.1e9) + 1, bytes_accessed=1, transcendentals=0),
        **more,
    )


def side_by_side(*refs):
    return jnp.concatenate([ref[j] for ref in refs for j in range(3)], axis=1)


def layer_norm(x):
    center = x - jnp.mean(x, axis=-1, keepdims=True)
    rstd = lax.rsqrt(jnp.mean(center * center, axis=-1, keepdims=True) + 1e-06)
    return center * rstd, rstd


def modulate_kernel(video_ref, text_ref, mod_ref, h_ref):
    shift, scale = mod_ref[0:1, :], 1.0 + mod_ref[1:2, :]
    vrows = video_ref.shape[0]
    for i in range(0, vrows, 16):
        normed, _ = layer_norm(video_ref[i : i + 16, :].astype(F))
        h_ref[i : i + 16, :] = (normed * scale + shift).astype(BF)
    normed, _ = layer_norm(text_ref[...].astype(F))
    h_ref[vrows:, :] = (normed * scale + shift).astype(BF)


def split_kernel(cut, y_ref, a_ref, b_ref, yt_ref, yl_ref, at_ref, bl_ref, m_ref):
    part = y_ref.shape[0] - cut
    yt_ref[...] = y_ref[:cut, :]
    yl_ref[...] = y_ref[cut:, :]
    at_ref[...] = a_ref[:cut, :]
    bl_ref[...] = b_ref[cut:, :]
    m_ref[:part, :] = a_ref[cut:, :]
    m_ref[part:, :] = b_ref[:cut, :]


def qkv_kernel(pieces, *refs):
    own_w, sib_w = refs[pieces : pieces + 2]
    h_ref, own_ref, sib_ref, acc = refs[pieces + 2 :]
    h = jnp.concatenate([ref[...] for ref in refs[:pieces]], axis=0)
    h_ref[...] = h
    w = side_by_side(own_w, sib_w)
    got = jnp.dot(h, w, preferred_element_type=F)
    step = pl.program_id(0)

    @pl.when(step == 0)
    def _():
        acc[...] = got

    @pl.when(step > 0)
    def _():
        acc[...] += got

    @pl.when(step == pl.num_programs(0) - 1)
    def _():
        cols = own_ref.shape[1]
        own_ref[...] = acc[:, :cols].astype(BF)
        sib_ref[...] = acc[:, cols:].astype(BF)


def d_attn_kernel(video_ref, text_ref, gate_ref, w_ref, out_ref, d_out):
    @pl.when(pl.program_id(0) == 0)
    def _():
        vrows = video_ref.shape[0]
        d_out[0:vrows, :] = (video_ref[...].astype(F) * gate_ref[...]).astype(BF)
        d_out[vrows:, :] = (text_ref[...].astype(F) * gate_ref[...]).astype(BF)

    got = lax.dot_general(d_out[...], w_ref[...], NT, preferred_element_type=F)
    for j in range(out_ref.shape[0]):
        out_ref[j] = got[:, j * HD : (j + 1) * HD].astype(BF)


def out_kernel(attn_ref, w_ref, video_ref, text_ref, dv_ref, dt_ref, gate_ref, ov_ref, ot_ref, dg_ref, tok):
    rows = tok.shape[0]

    @pl.when(pl.program_id(0) == 0)
    def _():
        for j in range(attn_ref.shape[0]):
            tok[:, j * HD : (j + 1) * HD] = attn_ref[j, 0:rows, :]

    out = jnp.dot(tok[...], w_ref[...], preferred_element_type=F)
    vrows = video_ref.shape[0]
    top, low = out[:vrows], out[vrows:]
    gate = gate_ref[...]
    ov_ref[...] = (video_ref[...].astype(F) + gate * top).astype(BF)
    ot_ref[...] = (text_ref[...].astype(F) + gate * low).astype(BF)
    dg_ref[...] = jnp.sum(dv_ref[...].astype(F) * top, axis=0, keepdims=True) + jnp.sum(
        dt_ref[...].astype(F) * low, axis=0, keepdims=True
    )


def far_kernel(cut, own_ref, sib_ref, wo_ref, ws_ref, yct_ref, ycl_ref, m1_ref, m2_ref, m_ref):
    d = jnp.concatenate([own_ref[...], sib_ref[...]], axis=1)
    w = side_by_side(wo_ref, ws_ref)
    got = lax.dot_general(d, w, NT, preferred_element_type=F)
    rows = got.shape[0] // 4
    c, ya, yb, yc = (got[i * rows : (i + 1) * rows] for i in range(4))
    yct_ref[...] = yc[:cut].astype(BF)
    ycl_ref[...] = yc[cut:].astype(BF)
    m1_ref[...] = jnp.concatenate([ya[:cut], c[:cut]], axis=0).astype(BF)
    m2_ref[...] = jnp.concatenate([yb[cut:], c[cut:]], axis=0).astype(BF)
    m_ref[...] = jnp.concatenate([ya[cut:], yb[:cut]], axis=0).astype(BF)


def add_kernel(base_ref, got_ref, out_ref):
    n = got_ref.shape[0]
    out_ref[:n, :] = (base_ref[:n, :].astype(F) + got_ref[...].astype(F)).astype(BF)
    out_ref[n:, :] = base_ref[n:, :]


def sums_kernel(cut, y_ref, a_ref, b_ref, r1_ref, r2_ref, r3_ref, oy_ref, oa_ref, ob_ref):
    part = y_ref.shape[0] - cut
    r1, r2, r3 = (ref[...].astype(F) for ref in (r1_ref, r2_ref, r3_ref))
    parts = (
        (y_ref, oy_ref, r1[:cut], r2[:part]),
        (a_ref, oa_ref, r1[cut:], r3[:part]),
        (b_ref, ob_ref, r3[part:], r2[part:]),
    )
    for ref, out, top, low in parts:
        out[...] = (ref[...].astype(F) + jnp.concatenate([top, low], axis=0)).astype(BF)


def near_kernel(own_ref, sib_ref, wo_ref, ws_ref, o_ref, y_ref, a_ref, b_ref):
    d = jnp.concatenate([own_ref[...], sib_ref[...]], axis=1)
    w = side_by_side(wo_ref, ws_ref)
    got = lax.dot_general(d, w, NT, preferred_element_type=F)
    rows = got.shape[0] // 4
    for i, ref in enumerate((o_ref, y_ref, a_ref, b_ref)):
        ref[...] = got[i * rows : (i + 1) * rows].astype(BF)


def grad_w_kernel(place_ref, one_ref, two_ref, own_ref, sib_ref, own_out, sib_out):
    h = jnp.concatenate([one_ref[...], two_ref[...]], axis=0)
    d = jnp.concatenate([own_ref[...], sib_ref[...]], axis=1)
    got = lax.dot_general(h, d, TN, preferred_element_type=F)
    wide, cols = own_out.shape[3], own_ref.shape[1]
    count = h.shape[1] // wide
    for i in range(count):
        at = (lax.rem(pl.program_id(0) * count, 4) + i - place_ref[0]) % 4
        for j in range(3):
            piece = got[i * wide : (i + 1) * wide]
            own_out[at, 0, j] = piece[:, j * HD : (j + 1) * HD].astype(BF)
            sib_out[at, 0, j] = piece[:, cols + j * HD : cols + (j + 1) * HD].astype(BF)


def gain_terms(values):
    high = values.astype(BF).astype(F)
    mid = (values - high).astype(BF).astype(F)
    low = values - high - mid
    pad = jnp.zeros((2, HD), F)
    return jnp.concatenate([high, mid, low, pad], axis=0).astype(BF)


def gain_value(terms):
    terms = terms.astype(F)
    return terms[0:2] + terms[2:4] + terms[4:6]


def both(own_ref, got_ref, k):
    total = own_ref[0, k].astype(F) + got_ref[0, k].astype(F)
    return total.reshape(total.shape[0] * total.shape[1], total.shape[2])


def far_section_kernel(own_ref, got_ref, attn_ref, f0_ref, f1_ref, gain_ref):
    flat = f0_ref.shape[0] - 8
    gains = gain_value(jnp.sum(attn_ref[...].astype(F), axis=0))
    for k, ref in enumerate((f0_ref, f1_ref)):
        ref[0:flat, :] = both(own_ref, got_ref, k).astype(BF)
        ref[flat:, :] = gain_terms(gains)
    gain_ref[...] = gains


def near_section_kernel(ao_ref, ag_ref, bo_ref, bg_ref, ga_ref, gb_ref, gain_ref, sa_ref, sb_ref, sum_ref):
    flat = ga_ref.shape[0] - 8
    sa_ref[0:flat, :] = both(ao_ref, ag_ref, 0).astype(BF)
    sa_ref[flat : 2 * flat, :] = (both(ao_ref, ag_ref, 1) + ga_ref[0:flat, :].astype(F)).astype(BF)
    sa_ref[2 * flat :, :] = ga_ref[flat:, :]
    sb_ref[0:flat, :] = (both(bo_ref, bg_ref, 0) + gb_ref[0:flat, :].astype(F)).astype(BF)
    sb_ref[flat:, :] = both(bo_ref, bg_ref, 1).astype(BF)
    sum_ref[...] = gain_ref[...] + gain_value(ga_ref[flat:, :]) + gain_value(gb_ref[flat:, :])


def own_section_kernel(own_ref, got_ref, a_ref, b_ref, gain_ref, keep_ref, give_ref, sum_ref):
    flat = keep_ref.shape[0]
    keep = both(own_ref, got_ref, 0)
    give = both(own_ref, got_ref, 1)
    keep_ref[...] = keep + a_ref[0:flat, :].astype(F) + b_ref[0:flat, :].astype(F)
    give += a_ref[flat : 2 * flat, :].astype(F) + b_ref[flat : 2 * flat, :].astype(F)
    give_ref[0:flat, :] = give.astype(BF)
    gains = gain_ref[...] + gain_value(a_ref[2 * flat :, :])
    give_ref[flat:, :] = gain_terms(gains)
    sum_ref[...] = gains


def tail_kernel(o_ref, ra_ref, rb_ref, ry_ref, video_ref, text_ref, dv_ref, dt_ref, mod_ref, dg_ref, gv_ref, gt_ref, m_ref):
    scale = 1.0 + mod_ref[1:2, :]
    vrows = video_ref.shape[0]
    first = jnp.zeros((8, scale.shape[1]), F)
    second = first
    everything = lambda at, n: (
        o_ref[at : at + n, :].astype(F)
        + ra_ref[at : at + n, :].astype(F)
        + rb_ref[at : at + n, :].astype(F)
        + ry_ref[at : at + n, :].astype(F)
    )
    fold = lambda v: jnp.sum(v.reshape(v.shape[0] // 8, 8, v.shape[1]), axis=0)
    pieces = [(i, 16, video_ref, dv_ref, gv_ref, i) for i in range(0, vrows, 16)]
    pieces.append((vrows, text_ref.shape[0], text_ref, dt_ref, gt_ref, 0))
    for at, n, x_ref, dy_ref, g_ref, lo in pieces:
        d_h = everything(at, n)
        normed, rstd = layer_norm(x_ref[lo : lo + n, :].astype(F))
        t = d_h * scale
        back = rstd * (
            t
            - jnp.mean(t, axis=-1, keepdims=True)
            - normed * jnp.mean(t * normed, axis=-1, keepdims=True)
        )
        g_ref[lo : lo + n, :] = (dy_ref[lo : lo + n, :].astype(F) + back).astype(BF)
        first += fold(d_h)
        second += fold(d_h * normed)
    rows = [jnp.sum(v, axis=0, keepdims=True) for v in (first, second)] + [dg_ref[...]]
    m = jnp.concatenate(rows, axis=0).astype(BF)
    m_ref[...] = jnp.broadcast_to(m[None], m_ref.shape)


def rms(x):
    r = lax.rsqrt(jnp.mean(x * x, axis=-1, keepdims=True) + 1e-6)
    return x * r, r


def rms_back(t, xh, r):
    return r * (t - xh * jnp.mean(t * xh, axis=-1, keepdims=True))


def attn_kernel(
    rows, order_ref, q1_ref, q2_ref, s1_ref, s2_ref, bias_ref, do_ref, gq_ref, gk_ref,
    attn_ref, own_ref, give_ref, q_s, kn_s, v_s, dq_s, dk_s, dv_s, gain_s,
):
    block = q1_ref.shape[0]
    parts = (q1_ref, q2_ref, s1_ref, s2_ref)
    outs = ((own_ref, 0), (own_ref, block), (give_ref, 0), (give_ref, block))
    per = block // rows
    scale = HD**-0.5
    step = pl.program_id(0)
    gq, gk = gq_ref[...], gk_ref[...]

    @pl.when(step == 0)
    def _():
        for i, ref in enumerate(parts):
            at = slice(i * block, (i + 1) * block)
            q_s[at, :] = ref[:, 0:HD]
            xh, _ = rms(ref[:, HD : 2 * HD].astype(F))
            kn_s[at, :] = (xh * gk).astype(BF)
            v_s[at, :] = ref[:, 2 * HD : 3 * HD]
        dk_s[...] = jnp.zeros_like(dk_s)
        dv_s[...] = jnp.zeros_like(dv_s)
        gain_s[...] = jnp.zeros_like(gain_s)

    here = pl.ds(pl.multiple_of(step * block, 16), block)
    xh, r = rms(q_s[here, :].astype(F))
    qn = (xh * (gq * scale)).astype(BF)
    s = lax.dot_general(qn, kn_s[...], NT, preferred_element_type=F) + bias_ref[...]
    e = jnp.exp(s)
    linv = 1.0 / jnp.sum(e, axis=-1, keepdims=True)
    eb = e.astype(BF)
    o = jnp.dot(eb, v_s[...], preferred_element_type=F) * linv
    do = jnp.concatenate(
        [do_ref[order_ref[step * per + j]].astype(F) for j in range(per)], axis=0
    )
    for j in range(per):
        attn_ref[order_ref[step * per + j], 0:rows, :] = o[j * rows : (j + 1) * rows].astype(BF)
    dn = do * linv
    dnb = dn.astype(BF)
    delta = jnp.sum(dn * o, axis=-1, keepdims=True)
    dp = lax.dot_general(dnb, v_s[...], NT, preferred_element_type=F)
    ds = (e * (dp - delta)).astype(BF)
    dq = jnp.dot(ds, kn_s[...], preferred_element_type=F)
    dk_s[...] += lax.dot_general(ds, qn, TN, preferred_element_type=F)
    dv_s[...] += lax.dot_general(eb, dnb, TN, preferred_element_type=F)
    gain_s[0:1, :] += jnp.sum(dq * xh, axis=0, keepdims=True) * scale
    dq_s[here, :] = rms_back(dq * (gq * scale), xh, r).astype(BF)

    @pl.when(step == 3)
    def _():
        for i, ref in enumerate(parts):
            out, at = outs[i]
            out[at : at + block, 0:HD] = dq_s[i * block : (i + 1) * block, :]
            xh, r = rms(ref[:, HD : 2 * HD].astype(F))
            dk = dk_s[i * block : (i + 1) * block, :]
            gain_s[1:2, :] += jnp.sum(dk * xh, axis=0, keepdims=True)
            out[at : at + block, HD : 2 * HD] = rms_back(dk * gk, xh, r).astype(BF)
            out[at : at + block, 2 * HD :] = dv_s[i * block : (i + 1) * block, :].astype(BF)
        gains = gain_s[...]
        high = gains.astype(BF).astype(F)
        low = (gains - high).astype(BF).astype(F)
        rest = gains - high - low
        tail = jnp.concatenate([high[0:2], low[0:2], rest[0:2], jnp.zeros((2, HD), F)], axis=0)
        attn_ref[:, rows:, :] = jnp.broadcast_to(tail.astype(BF)[None], (attn_ref.shape[0], 8, HD))


def ring(values, axis, distance):
    size = lax.axis_size(axis)
    return lax.ppermute(values, axis, [(i, (i + distance) % size) for i in range(size)])


def tie(values, *after):
    return lax.optimization_barrier((values, *after))[0]


def per_device(
    video, text, prompt_len, modulation, q_gain, k_gain, w_qkv, w_out, cot_video, cot_text
):
    video, text, cot_video, cot_text, modulation = (
        a[0] for a in (video, text, cot_video, cot_text, modulation)
    )
    vrows, trows = video.shape[0], text.shape[0]
    rows, width = vrows + trows, video.shape[1]
    heads = w_out.shape[0] // HD
    cols = 3 * HD
    yi, zi, ci = (lax.axis_index(a) for a in SEQ)
    zp = functools.partial(ring, axis="z", distance=1)
    zm = functools.partial(ring, axis="z", distance=-1)
    yy = functools.partial(ring, axis="y", distance=1)
    cc = functools.partial(ring, axis="core", distance=1)
    gate = modulation[2:3]
    cut = 64
    part = rows - cut

    h = call(modulate_kernel, shape((rows, width)))(video, text, modulation)
    w_own = jnp.transpose(w_qkv, (1, 0, 2))
    step = 2 * HD
    per = 4

    w_sib = cc(w_own)
    h_a, h_b, h_y = zp(h), zm(h), yy(h)
    d_attn = call(
        d_attn_kernel,
        shape((heads, rows, HD)),
        grid=(2 * per,),
        in_specs=[
            whole((vrows, width)),
            whole((trows, width)),
            whole((1, width)),
            pl.BlockSpec((step, width), lambda i: (i, 0)),
        ],
        out_specs=pl.BlockSpec((step // HD, rows, HD), lambda i: (i, 0, 0)),
        scratch_shapes=[pltpu.VMEM((rows, width), BF)],
    )(cot_video, cot_text, tie(gate, h, w_sib), w_out)
    y_t, y_l, a_t, b_l, m_ab = call(
        functools.partial(split_kernel, cut), tuple(shape((k, width)) for k in (cut, part, cut, part, rows))
    )(tie(h_y, d_attn), h_a, h_b)
    ya_t, yb_l = zp(y_t), zm(y_l)
    c_t, c_l = zp(a_t), zm(b_l)
    m_ab = yy(m_ab)
    n = len(PLACES) * rows
    block = n // 2
    strip = 1024

    def project(us, *parts):
        return call(
            functools.partial(qkv_kernel, len(parts)),
            (shape((block, width)), shape((block, cols)), shape((block, cols))),
            mib=56,
            us=us,
            grid=(width // strip,),
            in_specs=[pl.BlockSpec((k.shape[0], strip), lambda i: (0, i)) for k in parts]
            + [pl.BlockSpec((3, strip, HD), lambda i: (0, i, 0))] * 2,
            out_specs=[
                pl.BlockSpec((block, strip), lambda i: (0, i)),
                whole((block, cols)),
                whole((block, cols)),
            ],
            scratch_shapes=[pltpu.VMEM((block, 2 * cols), F)],
        )(*parts, w_own, w_sib)

    h_one, own_one, sib_one = project(0, h, h_y, h_a, h_b)
    yc_t, yc_l = zp(tie(ya_t, own_one)), zm(tie(yb_l, own_one))
    d_heads = lax.all_to_all(
        tie(d_attn, yc_t, yc_l), SEQ, split_axis=0, concat_axis=0, tiled=True
    )
    h_two, own_two, sib_two = project(0, c_t, c_l, ya_t, m_ab, yb_l, yc_t, yc_l)
    sib_two = cc(sib_two)
    sib_one = cc(tie(sib_one, own_two))

    order = jnp.stack(
        [(((yi + a) % 2) * 4 + (zi + b) % 4) * 2 + (ci + k) % 2 for k in (0, 1) for a, b in PLACES]
    ).astype(jnp.int32)
    inner = jnp.arange(rows, dtype=jnp.int32)[None, :]
    valid = (inner < vrows) | (order[:, None] * trows + inner - vrows < prompt_len[0])
    bias = jnp.where(valid, 0.0, -1e30).astype(F).reshape(1, 2 * n)

    attn, d_own, d_give = call(
        functools.partial(attn_kernel, rows),
        (shape((heads, rows + 8, HD)), shape((n, cols)), shape((n, cols))),
        mib=56,
        grid_spec=pltpu.PrefetchScalarGridSpec(
            num_scalar_prefetch=1,
            grid=(4,),
            in_specs=[whole(a) for a in ((block, cols),) * 4]
            + [whole((1, 2 * n)), whole((heads, rows, HD)), whole((1, HD)), whole((1, HD))],
            out_specs=[whole((heads, rows + 8, HD)), whole((n, cols)), whole((n, cols))],
            scratch_shapes=[
                pltpu.VMEM((2 * n, HD), BF),
                pltpu.VMEM((2 * n, HD), BF),
                pltpu.VMEM((2 * n, HD), BF),
                pltpu.VMEM((2 * n, HD), BF),
                pltpu.VMEM((2 * n, HD), F),
                pltpu.VMEM((2 * n, HD), F),
                pltpu.VMEM((8, HD), F),
            ],
        ),
    )(order, own_one, own_two, sib_one, sib_two, bias, d_heads, q_gain[None], k_gain[None])

    d_sib = cc(d_give)

    xi, hi = lax.axis_index("x"), lax.axis_index("yh")
    wide = width // 8
    here = jnp.stack([xi - 4, hi - 2]).astype(jnp.int32)

    attn_tok = lax.all_to_all(attn, SEQ, split_axis=0, concat_axis=0, tiled=True)
    strips = lambda count: pl.BlockSpec((count, strip), lambda i: (0, i))
    sizes = (cut, part, 2 * cut, 2 * part, rows)
    half_specs = lambda at: [
        pl.BlockSpec((block, cols), lambda i: (at, 0)),
        pl.BlockSpec((block, cols), lambda i: (at, 0)),
        pl.BlockSpec((3, strip, HD), lambda i: (0, i, 0)),
        pl.BlockSpec((3, strip, HD), lambda i: (0, i, 0)),
    ]
    work = dict(grid=(width // strip,), mib=56)
    yc_t, yc_l, m_1, m_2, m_3 = call(
        functools.partial(far_kernel, cut),
        tuple(shape((k, width)) for k in sizes),
        in_specs=half_specs(1),
        out_specs=[strips(k) for k in sizes],
        **work,
    )(d_own, d_sib, w_own, w_sib)
    r_ya, r_yb = zm(yc_t), zp(yc_l)
    r_3 = yy(m_3)
    g_own, g_sib = call(
        grad_w_kernel,
        (shape((4, 2, 3, wide, HD)),) * 2,
        us=12,
        mib=56,
        grid_spec=pltpu.PrefetchScalarGridSpec(
            num_scalar_prefetch=1,
            grid=(4,),
            in_specs=[pl.BlockSpec((block, 2 * wide), lambda i, p: (0, i))] * 2
            + [whole((n, cols))] * 2,
            out_specs=[
                pl.BlockSpec((4, 1, 3, wide, HD), lambda i, p: (0, (i // 2 - p[1]) % 2, 0, 0, 0))
            ]
            * 2,
        ),
    )(tie(here, m_3), h_one, h_two, d_own, d_sib)

    p_o, p_y, p_a, p_b = call(
        near_kernel,
        (shape((rows, width)),) * 4,
        in_specs=half_specs(0),
        out_specs=[strips(rows)] * 4,
        us=30,
        **work,
    )(tie(d_own, m_3), d_sib, w_own, w_sib)

    thirds = lambda count: pl.BlockSpec((count, width // 3), lambda i: (0, i))

    def add(base, got):
        return call(
            add_kernel,
            shape(base.shape),
            grid=(3,),
            in_specs=[thirds(base.shape[0]), thirds(got.shape[0])],
            out_specs=thirds(base.shape[0]),
        )(base, got)

    r_1, r_2 = zm(add(tie(m_1, g_own), r_ya)), zp(add(tie(m_2, g_own), r_yb))
    g_got = cc(g_sib)
    flat = 3 * wide
    pick = lambda r: [pl.BlockSpec((1, 2, 3, wide, HD), lambda i: (r, 0, 0, 0, 0))] * 2
    two = shape((2, HD), F)
    far_0, far_1, gains = call(
        far_section_kernel,
        (shape((flat + 8, HD)), shape((flat + 8, HD)), two),
        grid=(1,),
        in_specs=pick(2) + [pl.BlockSpec((heads, 8, HD), lambda i: (0, rows // 8, 0))],
        out_specs=[whole((flat + 8, HD)), whole((flat + 8, HD)), whole((2, HD))],
    )(g_own, g_got, tie(attn_tok, p_o))
    got_b, got_a = ring(far_0, "x", -1), ring(far_1, "x", 1)
    p_y, p_a, p_b = call(
        functools.partial(sums_kernel, cut),
        (shape((rows, width)),) * 3,
        grid=(3,),
        in_specs=[thirds(k) for k in (rows, rows, rows, 2 * cut, 2 * part, rows)],
        out_specs=[thirds(rows)] * 3,
    )(
        tie(p_y, far_0, far_1), p_a, p_b, r_1, r_2, r_3
    )
    last_a, last_b, last_y = zm(p_a), zp(p_b), yy(p_y)

    send_a, send_b, gains = call(
        near_section_kernel,
        (shape((2 * flat + 8, HD)), shape((2 * flat, HD)), two),
        grid=(1,),
        in_specs=pick(1) + pick(3) + [whole((flat + 8, HD))] * 2 + [whole((2, HD))],
        out_specs=[whole((2 * flat + 8, HD)), whole((2 * flat, HD)), whole((2, HD))],
    )(g_own, g_got, g_own, g_got, got_a, got_b, gains)
    back_a, back_b = ring(send_a, "x", 1), ring(send_b, "x", -1)
    keep, give, gains = call(
        own_section_kernel,
        (shape((flat, HD), F), shape((flat + 8, HD)), two),
        grid=(1,),
        in_specs=pick(0) + [whole((2 * flat + 8, HD)), whole((2 * flat, HD)), whole((2, HD))],
        out_specs=[whole((flat, HD)), whole((flat + 8, HD)), whole((2, HD))],
    )(g_own, g_got, back_a, back_b, gains)
    got = ring(give, "yh", 1)
    grad_w = (keep + got[:flat].astype(F)).reshape(3, wide, HD)
    grad_w = jnp.transpose(grad_w, (1, 0, 2))
    last = got[flat:].astype(F)
    grad_gain = gains + last[0:2] + last[2:4] + last[4:6]

    out_video, out_text, d_gate = call(
        out_kernel,
        (shape((vrows, width)), shape((trows, width)), shape((1, width), F)),
        us=8,
        grid=(width // strip,),
        mib=56,
        in_specs=[
            whole((heads, rows + 8, HD)),
            pl.BlockSpec((heads * HD, strip), lambda i: (0, i)),
        ]
        + [strips(k) for k in (vrows, trows, vrows, trows, 1)],
        out_specs=[strips(k) for k in (vrows, trows, 1)],
        scratch_shapes=[pltpu.VMEM((rows, heads * HD), BF)],
    )(tie(attn_tok, p_y, send_a, send_b), w_out, video, text, cot_video, cot_text, gate)

    grad_video, grad_text, wide_mod = call(
        tail_kernel,
        (shape((vrows, width)), shape((trows, width)), shape((heads, 3, width))),
    )(tie(p_o, give), last_a, last_b, last_y, video, text, cot_video, cot_text, modulation, d_gate)
    grad_mod = jnp.sum(
        lax.all_to_all(wide_mod, SEQ, split_axis=0, concat_axis=0, tiled=True).astype(F), axis=0
    )
    return (
        out_video[None],
        out_text[None],
        grad_video[None],
        grad_text[None],
        grad_mod[None],
        grad_w,
        grad_gain,
    )


def solution(mesh):
    fine = Mesh(mesh.devices.reshape(2, 4, 2, 4, 2), EVERY)
    tokens = P(SECTION, SEQ, None)
    sample = P(SECTION, None, None)
    return jax.shard_map(
        per_device,
        mesh=fine,
        in_specs=(tokens, tokens, P(SECTION), sample, P(), P(), P(None, None, SEQ), P(), tokens, tokens),
        out_specs=(tokens, tokens, tokens, tokens, sample, P(SECTION, None, SEQ), P()),
        check_vma=False,
    )
```

```python
import functools
import jax
import jax.numpy as jnp
from jax import lax
from jax.experimental import pallas as pl
from jax.experimental.pallas import tpu as pltpu
from jax.sharding import Mesh
from jax.sharding import PartitionSpec as P

BF = jnp.bfloat16
F = jnp.float32
HD = 128
SEQ = ("y", "z", "core")
SECTION = ("yh", "x")
EVERY = SECTION + SEQ
NT = (((1,), (1,)), ((), ()))
TN = (((0,), (0,)), ((), ()))
PLACES = [(0, 0), (1, 0), (0, -1), (0, 1), (0, 2), (1, -1), (1, 1), (1, 2)]


def shape(dims, kind=BF):
    return jax.ShapeDtypeStruct(dims, kind)


def whole(dims):
    return pl.BlockSpec(dims, lambda *_: (0,) * len(dims))


def call(kernel, outs, mib=48, us=0, **more):
    return pl.pallas_call(
        kernel,
        out_shape=outs,
        compiler_params=pltpu.CompilerParams(vmem_limit_bytes=mib * 2**20),
        cost_estimate=pl.CostEstimate(flops=int(us * 1.1e9) + 1, bytes_accessed=1, transcendentals=0),
        **more,
    )


def side_by_side(*refs):
    return jnp.concatenate([ref[j] for ref in refs for j in range(3)], axis=1)


def layer_norm(x):
    center = x - jnp.mean(x, axis=-1, keepdims=True)
    rstd = lax.rsqrt(jnp.mean(center * center, axis=-1, keepdims=True) + 1e-06)
    return center * rstd, rstd


def modulate_kernel(video_ref, text_ref, mod_ref, h_ref):
    shift, scale = mod_ref[0:1, :], 1.0 + mod_ref[1:2, :]
    vrows = video_ref.shape[0]
    for i in range(0, vrows, 16):
        normed, _ = layer_norm(video_ref[i : i + 16, :].astype(F))
        h_ref[i : i + 16, :] = (normed * scale + shift).astype(BF)
    normed, _ = layer_norm(text_ref[...].astype(F))
    h_ref[vrows:, :] = (normed * scale + shift).astype(BF)


def split_kernel(cut, y_ref, a_ref, b_ref, yt_ref, yl_ref, at_ref, bl_ref, m_ref):
    part = y_ref.shape[0] - cut
    yt_ref[...] = y_ref[:cut, :]
    yl_ref[...] = y_ref[cut:, :]
    at_ref[...] = a_ref[:cut, :]
    bl_ref[...] = b_ref[cut:, :]
    m_ref[:part, :] = a_ref[cut:, :]
    m_ref[part:, :] = b_ref[:cut, :]


def qkv_kernel(pieces, *refs):
    own_w, sib_w = refs[pieces : pieces + 2]
    h_ref, own_ref, sib_ref, acc = refs[pieces + 2 :]
    h = jnp.concatenate([ref[...] for ref in refs[:pieces]], axis=0)
    h_ref[...] = h
    w = side_by_side(own_w, sib_w)
    got = jnp.dot(h, w, preferred_element_type=F)
    step = pl.program_id(0)

    @pl.when(step == 0)
    def _():
        acc[...] = got

    @pl.when(step > 0)
    def _():
        acc[...] += got

    @pl.when(step == pl.num_programs(0) - 1)
    def _():
        cols = own_ref.shape[1]
        own_ref[...] = acc[:, :cols].astype(BF)
        sib_ref[...] = acc[:, cols:].astype(BF)


def d_attn_kernel(video_ref, text_ref, gate_ref, w_ref, out_ref, d_out):
    @pl.when(pl.program_id(0) == 0)
    def _():
        vrows = video_ref.shape[0]
        d_out[0:vrows, :] = (video_ref[...].astype(F) * gate_ref[...]).astype(BF)
        d_out[vrows:, :] = (text_ref[...].astype(F) * gate_ref[...]).astype(BF)

    got = lax.dot_general(d_out[...], w_ref[...], NT, preferred_element_type=F)
    for j in range(out_ref.shape[0]):
        out_ref[j] = got[:, j * HD : (j + 1) * HD].astype(BF)


def out_kernel(attn_ref, w_ref, video_ref, text_ref, dv_ref, dt_ref, gate_ref, ov_ref, ot_ref, dg_ref, tok):
    rows = tok.shape[0]

    @pl.when(pl.program_id(0) == 0)
    def _():
        for j in range(attn_ref.shape[0]):
            tok[:, j * HD : (j + 1) * HD] = attn_ref[j, 0:rows, :]

    out = jnp.dot(tok[...], w_ref[...], preferred_element_type=F)
    vrows = video_ref.shape[0]
    top, low = out[:vrows], out[vrows:]
    gate = gate_ref[...]
    ov_ref[...] = (video_ref[...].astype(F) + gate * top).astype(BF)
    ot_ref[...] = (text_ref[...].astype(F) + gate * low).astype(BF)
    dg_ref[...] = jnp.sum(dv_ref[...].astype(F) * top, axis=0, keepdims=True) + jnp.sum(
        dt_ref[...].astype(F) * low, axis=0, keepdims=True
    )


def far_kernel(cut, own_ref, sib_ref, wo_ref, ws_ref, yct_ref, ycl_ref, m1_ref, m2_ref, m_ref):
    d = jnp.concatenate([own_ref[...], sib_ref[...]], axis=1)
    w = side_by_side(wo_ref, ws_ref)
    got = lax.dot_general(d, w, NT, preferred_element_type=F)
    rows = got.shape[0] // 4
    c, ya, yb, yc = (got[i * rows : (i + 1) * rows] for i in range(4))
    yct_ref[...] = yc[:cut].astype(BF)
    ycl_ref[...] = yc[cut:].astype(BF)
    m1_ref[...] = jnp.concatenate([ya[:cut], c[:cut]], axis=0).astype(BF)
    m2_ref[...] = jnp.concatenate([yb[cut:], c[cut:]], axis=0).astype(BF)
    m_ref[...] = jnp.concatenate([ya[cut:], yb[:cut]], axis=0).astype(BF)


def add_kernel(one_ref, two_ref, got1_ref, got2_ref, out1_ref, out2_ref):
    for base_ref, got_ref, out_ref in ((one_ref, got1_ref, out1_ref), (two_ref, got2_ref, out2_ref)):
        n = got_ref.shape[0]
        out_ref[:n, :] = (base_ref[:n, :].astype(F) + got_ref[...].astype(F)).astype(BF)
        out_ref[n:, :] = base_ref[n:, :]


def sums_kernel(cut, y_ref, a_ref, b_ref, r1_ref, r2_ref, r3_ref, oy_ref, oa_ref, ob_ref):
    part = y_ref.shape[0] - cut
    r1, r2, r3 = (ref[...].astype(F) for ref in (r1_ref, r2_ref, r3_ref))
    parts = (
        (y_ref, oy_ref, r1[:cut], r2[:part]),
        (a_ref, oa_ref, r1[cut:], r3[:part]),
        (b_ref, ob_ref, r3[part:], r2[part:]),
    )
    for ref, out, top, low in parts:
        out[...] = (ref[...].astype(F) + jnp.concatenate([top, low], axis=0)).astype(BF)


def near_kernel(own_ref, sib_ref, wo_ref, ws_ref, o_ref, y_ref, a_ref, b_ref):
    d = jnp.concatenate([own_ref[...], sib_ref[...]], axis=1)
    w = side_by_side(wo_ref, ws_ref)
    got = lax.dot_general(d, w, NT, preferred_element_type=F)
    rows = got.shape[0] // 4
    for i, ref in enumerate((o_ref, y_ref, a_ref, b_ref)):
        ref[...] = got[i * rows : (i + 1) * rows].astype(BF)


def grad_w_kernel(place_ref, one_ref, two_ref, own_ref, sib_ref, own_out, sib_out):
    h = jnp.concatenate([one_ref[...], two_ref[...]], axis=0)
    d = jnp.concatenate([own_ref[...], sib_ref[...]], axis=1)
    got = lax.dot_general(h, d, TN, preferred_element_type=F)
    wide, cols = own_out.shape[3], own_ref.shape[1]
    count = h.shape[1] // wide
    for i in range(count):
        at = (lax.rem(pl.program_id(0) * count, 4) + i - place_ref[0]) % 4
        for j in range(3):
            piece = got[i * wide : (i + 1) * wide]
            own_out[at, 0, j] = piece[:, j * HD : (j + 1) * HD].astype(BF)
            sib_out[at, 0, j] = piece[:, cols + j * HD : cols + (j + 1) * HD].astype(BF)


def gain_terms(values):
    high = values.astype(BF).astype(F)
    mid = (values - high).astype(BF).astype(F)
    low = values - high - mid
    pad = jnp.zeros((2, HD), F)
    return jnp.concatenate([high, mid, low, pad], axis=0).astype(BF)


def gain_value(terms):
    terms = terms.astype(F)
    return terms[0:2] + terms[2:4] + terms[4:6]


def both(own_ref, got_ref, k):
    total = own_ref[0, k].astype(F) + got_ref[0, k].astype(F)
    return total.reshape(total.shape[0] * total.shape[1], total.shape[2])


def far_section_kernel(own_ref, got_ref, attn_ref, f0_ref, f1_ref, gain_ref):
    flat = f0_ref.shape[0] - 8
    gains = gain_value(jnp.sum(attn_ref[...].astype(F), axis=0))
    for k, ref in enumerate((f0_ref, f1_ref)):
        ref[0:flat, :] = both(own_ref, got_ref, k).astype(BF)
        ref[flat:, :] = gain_terms(gains)
    gain_ref[...] = gains


def near_section_kernel(ao_ref, ag_ref, bo_ref, bg_ref, ga_ref, gb_ref, gain_ref, sa_ref, sb_ref, sum_ref):
    flat = ga_ref.shape[0] - 8
    sa_ref[0:flat, :] = both(ao_ref, ag_ref, 0).astype(BF)
    sa_ref[flat : 2 * flat, :] = (both(ao_ref, ag_ref, 1) + ga_ref[0:flat, :].astype(F)).astype(BF)
    sa_ref[2 * flat :, :] = ga_ref[flat:, :]
    sb_ref[0:flat, :] = (both(bo_ref, bg_ref, 0) + gb_ref[0:flat, :].astype(F)).astype(BF)
    sb_ref[flat:, :] = both(bo_ref, bg_ref, 1).astype(BF)
    sum_ref[...] = gain_ref[...] + gain_value(ga_ref[flat:, :]) + gain_value(gb_ref[flat:, :])


def own_section_kernel(own_ref, got_ref, a_ref, b_ref, gain_ref, keep_ref, give_ref, sum_ref):
    flat = keep_ref.shape[0]
    keep = both(own_ref, got_ref, 0)
    give = both(own_ref, got_ref, 1)
    keep_ref[...] = keep + a_ref[0:flat, :].astype(F) + b_ref[0:flat, :].astype(F)
    give += a_ref[flat : 2 * flat, :].astype(F) + b_ref[flat : 2 * flat, :].astype(F)
    give_ref[0:flat, :] = give.astype(BF)
    gains = gain_ref[...] + gain_value(a_ref[2 * flat :, :])
    give_ref[flat:, :] = gain_terms(gains)
    sum_ref[...] = gains


def tail_kernel(o_ref, ra_ref, rb_ref, ry_ref, video_ref, text_ref, dv_ref, dt_ref, mod_ref, dg_ref, gv_ref, gt_ref, m_ref):
    scale = 1.0 + mod_ref[1:2, :]
    vrows = video_ref.shape[0]
    first = jnp.zeros((8, scale.shape[1]), F)
    second = first
    everything = lambda at, n: (
        o_ref[at : at + n, :].astype(F)
        + ra_ref[at : at + n, :].astype(F)
        + rb_ref[at : at + n, :].astype(F)
        + ry_ref[at : at + n, :].astype(F)
    )
    fold = lambda v: jnp.sum(v.reshape(v.shape[0] // 8, 8, v.shape[1]), axis=0)
    pieces = [(i, 16, video_ref, dv_ref, gv_ref, i) for i in range(0, vrows, 16)]
    pieces.append((vrows, text_ref.shape[0], text_ref, dt_ref, gt_ref, 0))
    for at, n, x_ref, dy_ref, g_ref, lo in pieces:
        d_h = everything(at, n)
        normed, rstd = layer_norm(x_ref[lo : lo + n, :].astype(F))
        t = d_h * scale
        back = rstd * (
            t
            - jnp.mean(t, axis=-1, keepdims=True)
            - normed * jnp.mean(t * normed, axis=-1, keepdims=True)
        )
        g_ref[lo : lo + n, :] = (dy_ref[lo : lo + n, :].astype(F) + back).astype(BF)
        first += fold(d_h)
        second += fold(d_h * normed)
    rows = [jnp.sum(v, axis=0, keepdims=True) for v in (first, second)] + [dg_ref[...]]
    m = jnp.concatenate(rows, axis=0).astype(BF)
    m_ref[...] = jnp.broadcast_to(m[None], m_ref.shape)


def rms(x):
    r = lax.rsqrt(jnp.mean(x * x, axis=-1, keepdims=True) + 1e-6)
    return x * r, r


def rms_back(t, xh, r):
    return r * (t - xh * jnp.mean(t * xh, axis=-1, keepdims=True))


def attn_kernel(
    rows, order_ref, q1_ref, q2_ref, s1_ref, s2_ref, bias_ref, do_ref, gq_ref, gk_ref,
    attn_ref, own_ref, give_ref, q_s, kn_s, v_s, dq_s, dk_s, dv_s, gain_s,
):
    part = q1_ref.shape[0]
    block = 2 * part
    parts = (q1_ref, q2_ref, s1_ref, s2_ref)
    outs = ((own_ref, 0), (own_ref, part), (give_ref, 0), (give_ref, part))
    per = block // rows
    scale = HD**-0.5
    step = pl.program_id(0)
    gq, gk = gq_ref[...], gk_ref[...]

    @pl.when(step == 0)
    def _():
        for i, ref in enumerate(parts):
            at = slice(i * part, (i + 1) * part)
            q_s[at, :] = ref[:, 0:HD]
            xh, _ = rms(ref[:, HD : 2 * HD].astype(F))
            kn_s[at, :] = (xh * gk).astype(BF)
            v_s[at, :] = ref[:, 2 * HD : 3 * HD]
        dk_s[...] = jnp.zeros_like(dk_s)
        dv_s[...] = jnp.zeros_like(dv_s)
        gain_s[...] = jnp.zeros_like(gain_s)

    here = pl.ds(pl.multiple_of(step * block, 16), block)
    xh, r = rms(q_s[here, :].astype(F))
    qn = (xh * (gq * scale)).astype(BF)
    s = lax.dot_general(qn, kn_s[...], NT, preferred_element_type=F) + bias_ref[...]
    e = jnp.exp(s)
    linv = 1.0 / jnp.sum(e, axis=-1, keepdims=True)
    eb = e.astype(BF)
    o = jnp.dot(eb, v_s[...], preferred_element_type=F) * linv
    do = jnp.concatenate(
        [do_ref[order_ref[step * per + j]].astype(F) for j in range(per)], axis=0
    )
    for j in range(per):
        attn_ref[order_ref[step * per + j], 0:rows, :] = o[j * rows : (j + 1) * rows].astype(BF)
    dn = do * linv
    dnb = dn.astype(BF)
    delta = jnp.sum(dn * o, axis=-1, keepdims=True)
    dp = lax.dot_general(dnb, v_s[...], NT, preferred_element_type=F)
    ds = (e * (dp - delta)).astype(BF)
    dq = jnp.dot(ds, kn_s[...], preferred_element_type=F)
    dk_s[...] += lax.dot_general(ds, qn, TN, preferred_element_type=F)
    dv_s[...] += lax.dot_general(eb, dnb, TN, preferred_element_type=F)
    gain_s[0:1, :] += jnp.sum(dq * xh, axis=0, keepdims=True) * scale
    dq_s[here, :] = rms_back(dq * (gq * scale), xh, r).astype(BF)

    @pl.when(step == 1)
    def _():
        for i, ref in enumerate(parts):
            out, at = outs[i]
            out[at : at + part, 0:HD] = dq_s[i * part : (i + 1) * part, :]
            xh, r = rms(ref[:, HD : 2 * HD].astype(F))
            dk = dk_s[i * part : (i + 1) * part, :]
            gain_s[1:2, :] += jnp.sum(dk * xh, axis=0, keepdims=True)
            out[at : at + part, HD : 2 * HD] = rms_back(dk * gk, xh, r).astype(BF)
            out[at : at + part, 2 * HD :] = dv_s[i * part : (i + 1) * part, :].astype(BF)
        gains = gain_s[...]
        high = gains.astype(BF).astype(F)
        low = (gains - high).astype(BF).astype(F)
        rest = gains - high - low
        tail = jnp.concatenate([high[0:2], low[0:2], rest[0:2], jnp.zeros((2, HD), F)], axis=0)
        attn_ref[:, rows:, :] = jnp.broadcast_to(tail.astype(BF)[None], (attn_ref.shape[0], 8, HD))


def ring(values, axis, distance):
    size = lax.axis_size(axis)
    return lax.ppermute(values, axis, [(i, (i + distance) % size) for i in range(size)])


def tie(values, *after):
    return lax.optimization_barrier((values, *after))[0]


def per_device(
    video, text, prompt_len, modulation, q_gain, k_gain, w_qkv, w_out, cot_video, cot_text
):
    video, text, cot_video, cot_text, modulation = (
        a[0] for a in (video, text, cot_video, cot_text, modulation)
    )
    vrows, trows = video.shape[0], text.shape[0]
    rows, width = vrows + trows, video.shape[1]
    heads = w_out.shape[0] // HD
    cols = 3 * HD
    yi, zi, ci = (lax.axis_index(a) for a in SEQ)
    zp = functools.partial(ring, axis="z", distance=1)
    zm = functools.partial(ring, axis="z", distance=-1)
    yy = functools.partial(ring, axis="y", distance=1)
    cc = functools.partial(ring, axis="core", distance=1)
    gate = modulation[2:3]
    cut = 64
    part = rows - cut

    h = call(modulate_kernel, shape((rows, width)))(video, text, modulation)
    w_own = jnp.transpose(w_qkv, (1, 0, 2))
    step = 2 * HD
    per = 4

    w_sib = cc(w_own)
    h_a, h_b, h_y = zp(h), zm(h), yy(h)
    d_attn = call(
        d_attn_kernel,
        shape((heads, rows, HD)),
        grid=(2 * per,),
        in_specs=[
            whole((vrows, width)),
            whole((trows, width)),
            whole((1, width)),
            pl.BlockSpec((step, width), lambda i: (i, 0)),
        ],
        out_specs=pl.BlockSpec((step // HD, rows, HD), lambda i: (i, 0, 0)),
        scratch_shapes=[pltpu.VMEM((rows, width), BF)],
    )(cot_video, cot_text, tie(gate, h, w_sib), w_out)
    y_t, y_l, a_t, b_l, m_ab = call(
        functools.partial(split_kernel, cut), tuple(shape((k, width)) for k in (cut, part, cut, part, rows))
    )(tie(h_y, d_attn), h_a, h_b)
    ya_t, yb_l = zp(y_t), zm(y_l)
    c_t, c_l = zp(a_t), zm(b_l)
    m_ab = yy(m_ab)
    n = len(PLACES) * rows
    block = n // 2
    strip = 1024

    def project(us, *parts):
        return call(
            functools.partial(qkv_kernel, len(parts)),
            (shape((block, width)), shape((block, cols)), shape((block, cols))),
            mib=56,
            us=us,
            grid=(width // strip,),
            in_specs=[pl.BlockSpec((k.shape[0], strip), lambda i: (0, i)) for k in parts]
            + [pl.BlockSpec((3, strip, HD), lambda i: (0, i, 0))] * 2,
            out_specs=[
                pl.BlockSpec((block, strip), lambda i: (0, i)),
                whole((block, cols)),
                whole((block, cols)),
            ],
            scratch_shapes=[pltpu.VMEM((block, 2 * cols), F)],
        )(*parts, w_own, w_sib)

    h_one, own_one, sib_one = project(0, h, h_y, h_a, h_b)
    yc_t, yc_l = zp(tie(ya_t, own_one)), zm(tie(yb_l, own_one))
    d_heads = lax.all_to_all(
        tie(d_attn, yc_t, yc_l), SEQ, split_axis=0, concat_axis=0, tiled=True
    )
    h_two, own_two, sib_two = project(0, c_t, c_l, ya_t, m_ab, yb_l, yc_t, yc_l)
    sib_two = cc(sib_two)
    sib_one = cc(tie(sib_one, own_two))

    order = jnp.stack(
        [(((yi + a) % 2) * 4 + (zi + b) % 4) * 2 + (ci + k) % 2 for k in (0, 1) for a, b in PLACES]
    ).astype(jnp.int32)
    inner = jnp.arange(rows, dtype=jnp.int32)[None, :]
    valid = (inner < vrows) | (order[:, None] * trows + inner - vrows < prompt_len[0])
    bias = jnp.where(valid, 0.0, -1e30).astype(F).reshape(1, 2 * n)

    attn, d_own, d_give = call(
        functools.partial(attn_kernel, rows),
        (shape((heads, rows + 8, HD)), shape((n, cols)), shape((n, cols))),
        mib=56,
        grid_spec=pltpu.PrefetchScalarGridSpec(
            num_scalar_prefetch=1,
            grid=(2,),
            in_specs=[whole(a) for a in ((block, cols),) * 4]
            + [whole((1, 2 * n)), whole((heads, rows, HD)), whole((1, HD)), whole((1, HD))],
            out_specs=[whole((heads, rows + 8, HD)), whole((n, cols)), whole((n, cols))],
            scratch_shapes=[
                pltpu.VMEM((2 * n, HD), BF),
                pltpu.VMEM((2 * n, HD), BF),
                pltpu.VMEM((2 * n, HD), BF),
                pltpu.VMEM((2 * n, HD), BF),
                pltpu.VMEM((2 * n, HD), F),
                pltpu.VMEM((2 * n, HD), F),
                pltpu.VMEM((8, HD), F),
            ],
        ),
    )(order, own_one, own_two, sib_one, sib_two, bias, d_heads, q_gain[None], k_gain[None])

    d_sib = cc(d_give)

    xi, hi = lax.axis_index("x"), lax.axis_index("yh")
    wide = width // 8
    here = jnp.stack([xi - 4, hi - 2]).astype(jnp.int32)

    attn_tok = lax.all_to_all(attn, SEQ, split_axis=0, concat_axis=0, tiled=True)
    strips = lambda count: pl.BlockSpec((count, strip), lambda i: (0, i))
    sizes = (cut, part, 2 * cut, 2 * part, rows)
    half_specs = lambda at: [
        pl.BlockSpec((block, cols), lambda i: (at, 0)),
        pl.BlockSpec((block, cols), lambda i: (at, 0)),
        pl.BlockSpec((3, strip, HD), lambda i: (0, i, 0)),
        pl.BlockSpec((3, strip, HD), lambda i: (0, i, 0)),
    ]
    work = dict(grid=(width // strip,), mib=56)
    yc_t, yc_l, m_1, m_2, m_3 = call(
        functools.partial(far_kernel, cut),
        tuple(shape((k, width)) for k in sizes),
        in_specs=half_specs(1),
        out_specs=[strips(k) for k in sizes],
        **work,
    )(d_own, d_sib, w_own, w_sib)
    r_ya, r_yb = zm(yc_t), zp(yc_l)
    r_3 = yy(m_3)
    g_own, g_sib = call(
        grad_w_kernel,
        (shape((4, 2, 3, wide, HD)),) * 2,
        us=20,
        mib=56,
        grid_spec=pltpu.PrefetchScalarGridSpec(
            num_scalar_prefetch=1,
            grid=(4,),
            in_specs=[pl.BlockSpec((block, 2 * wide), lambda i, p: (0, i))] * 2
            + [whole((n, cols))] * 2,
            out_specs=[
                pl.BlockSpec((4, 1, 3, wide, HD), lambda i, p: (0, (i // 2 - p[1]) % 2, 0, 0, 0))
            ]
            * 2,
        ),
    )(tie(here, m_3), h_one, h_two, d_own, d_sib)

    p_o, p_y, p_a, p_b = call(
        near_kernel,
        (shape((rows, width)),) * 4,
        in_specs=half_specs(0),
        out_specs=[strips(rows)] * 4,
        us=30,
        **work,
    )(tie(d_own, m_3), d_sib, w_own, w_sib)

    thirds = lambda count: pl.BlockSpec((count, width // 3), lambda i: (0, i))

    m_1, m_2 = call(
        add_kernel,
        (shape((2 * cut, width)), shape((2 * part, width))),
        us=30,
        grid=(3,),
        in_specs=[thirds(k) for k in (2 * cut, 2 * part, cut, part)],
        out_specs=[thirds(2 * cut), thirds(2 * part)],
    )(tie(m_1, g_own), m_2, r_ya, r_yb)
    r_1, r_2 = zm(m_1), zp(m_2)
    g_got = cc(g_sib)
    flat = 3 * wide
    pick = lambda r: [pl.BlockSpec((1, 2, 3, wide, HD), lambda i: (r, 0, 0, 0, 0))] * 2
    two = shape((2, HD), F)
    far_0, far_1, gains = call(
        far_section_kernel,
        (shape((flat + 8, HD)), shape((flat + 8, HD)), two),
        grid=(1,),
        in_specs=pick(2) + [pl.BlockSpec((heads, 8, HD), lambda i: (0, rows // 8, 0))],
        out_specs=[whole((flat + 8, HD)), whole((flat + 8, HD)), whole((2, HD))],
    )(g_own, g_got, tie(attn_tok, m_1, m_2))
    got_b, got_a = ring(far_0, "x", -1), ring(far_1, "x", 1)
    send_a, send_b, gains = call(
        near_section_kernel,
        (shape((2 * flat + 8, HD)), shape((2 * flat, HD)), two),
        grid=(1,),
        in_specs=pick(1) + pick(3) + [whole((flat + 8, HD))] * 2 + [whole((2, HD))],
        out_specs=[whole((2 * flat + 8, HD)), whole((2 * flat, HD)), whole((2, HD))],
    )(g_own, g_got, g_own, g_got, got_a, got_b, tie(gains, p_o))
    p_y, p_a, p_b = call(
        functools.partial(sums_kernel, cut),
        (shape((rows, width)),) * 3,
        grid=(3,),
        in_specs=[thirds(k) for k in (rows, rows, rows, 2 * cut, 2 * part, rows)],
        out_specs=[thirds(rows)] * 3,
    )(
        tie(p_y, send_a, send_b), p_a, p_b, r_1, r_2, r_3
    )
    last_a, last_b, last_y = zm(p_a), zp(p_b), yy(p_y)

    back_a, back_b = ring(send_a, "x", 1), ring(send_b, "x", -1)
    keep, give, gains = call(
        own_section_kernel,
        (shape((flat, HD), F), shape((flat + 8, HD)), two),
        grid=(1,),
        in_specs=pick(0) + [whole((2 * flat + 8, HD)), whole((2 * flat, HD)), whole((2, HD))],
        out_specs=[whole((flat, HD)), whole((flat + 8, HD)), whole((2, HD))],
    )(g_own, g_got, back_a, back_b, gains)
    got = ring(give, "yh", 1)
    grad_w = (keep + got[:flat].astype(F)).reshape(3, wide, HD)
    grad_w = jnp.transpose(grad_w, (1, 0, 2))
    last = got[flat:].astype(F)
    grad_gain = gains + last[0:2] + last[2:4] + last[4:6]

    out_video, out_text, d_gate = call(
        out_kernel,
        (shape((vrows, width)), shape((trows, width)), shape((1, width), F)),
        us=8,
        grid=(width // strip,),
        mib=56,
        in_specs=[
            whole((heads, rows + 8, HD)),
            pl.BlockSpec((heads * HD, strip), lambda i: (0, i)),
        ]
        + [strips(k) for k in (vrows, trows, vrows, trows, 1)],
        out_specs=[strips(k) for k in (vrows, trows, 1)],
        scratch_shapes=[pltpu.VMEM((rows, heads * HD), BF)],
    )(tie(attn_tok, p_y), w_out, video, text, cot_video, cot_text, gate)

    grad_video, grad_text, wide_mod = call(
        tail_kernel,
        (shape((vrows, width)), shape((trows, width)), shape((heads, 3, width))),
    )(tie(p_o, give), last_a, last_b, last_y, video, text, cot_video, cot_text, modulation, d_gate)
    grad_mod = jnp.sum(
        lax.all_to_all(wide_mod, SEQ, split_axis=0, concat_axis=0, tiled=True).astype(F), axis=0
    )
    return (
        out_video[None],
        out_text[None],
        grad_video[None],
        grad_text[None],
        grad_mod[None],
        grad_w,
        grad_gain,
    )


def solution(mesh):
    fine = Mesh(mesh.devices.reshape(2, 4, 2, 4, 2), EVERY)
    tokens = P(SECTION, SEQ, None)
    sample = P(SECTION, None, None)
    return jax.shard_map(
        per_device,
        mesh=fine,
        in_specs=(tokens, tokens, P(SECTION), sample, P(), P(), P(None, None, SEQ), P(), tokens, tokens),
        out_specs=(tokens, tokens, tokens, tokens, sample, P(SECTION, None, SEQ), P()),
        check_vma=False,
    )
```

```python
import functools
import jax
import jax.numpy as jnp
from jax import lax
from jax.experimental import pallas as pl
from jax.experimental.pallas import tpu as pltpu
from jax.sharding import Mesh
from jax.sharding import PartitionSpec as P

BF = jnp.bfloat16
F = jnp.float32
HD = 128
SEQ = ("y", "z", "core")
SECTION = ("yh", "x")
EVERY = SECTION + SEQ
NT = (((1,), (1,)), ((), ()))
TN = (((0,), (0,)), ((), ()))
PLACES = [(0, 0), (1, 0), (0, -1), (0, 1), (0, 2), (1, -1), (1, 1), (1, 2)]


def shape(dims, kind=BF):
    return jax.ShapeDtypeStruct(dims, kind)


def whole(dims):
    return pl.BlockSpec(dims, lambda *_: (0,) * len(dims))


def call(kernel, outs, mib=48, us=0, **more):
    return pl.pallas_call(
        kernel,
        out_shape=outs,
        compiler_params=pltpu.CompilerParams(vmem_limit_bytes=mib * 2**20),
        cost_estimate=pl.CostEstimate(flops=int(us * 1.1e9) + 1, bytes_accessed=1, transcendentals=0),
        **more,
    )


def side_by_side(*refs):
    return jnp.concatenate([ref[j] for ref in refs for j in range(3)], axis=1)


def layer_norm(x):
    center = x - jnp.mean(x, axis=-1, keepdims=True)
    rstd = lax.rsqrt(jnp.mean(center * center, axis=-1, keepdims=True) + 1e-06)
    return center * rstd, rstd


def norm_kernel(video_ref, text_ref, out_ref):
    vrows = video_ref.shape[0]
    for i in range(0, vrows, 16):
        out_ref[i : i + 16, :] = layer_norm(video_ref[i : i + 16, :].astype(F))[0].astype(BF)
    out_ref[vrows:, :] = layer_norm(text_ref[...].astype(F))[0].astype(BF)


def split_kernel(cut, y_ref, a_ref, b_ref, yt_ref, yl_ref, at_ref, bl_ref, m_ref):
    part = y_ref.shape[0] - cut
    yt_ref[...] = y_ref[:cut, :]
    yl_ref[...] = y_ref[cut:, :]
    at_ref[...] = a_ref[:cut, :]
    bl_ref[...] = b_ref[cut:, :]
    m_ref[:part, :] = a_ref[cut:, :]
    m_ref[part:, :] = b_ref[:cut, :]


def qkv_kernel(pieces, *refs):
    own_w, sib_w, mod_ref = refs[pieces : pieces + 3]
    n_ref, own_ref, sib_ref, acc = refs[pieces + 3 :]
    normed = jnp.concatenate([ref[...] for ref in refs[:pieces]], axis=0)
    n_ref[...] = normed
    h = (normed.astype(F) * (1.0 + mod_ref[1:2, :]) + mod_ref[0:1, :]).astype(BF)
    w = side_by_side(own_w, sib_w)
    got = jnp.dot(h, w, preferred_element_type=F)
    step = pl.program_id(0)

    @pl.when(step == 0)
    def _():
        acc[...] = got

    @pl.when(step > 0)
    def _():
        acc[...] += got

    @pl.when(step == pl.num_programs(0) - 1)
    def _():
        cols = own_ref.shape[1]
        own_ref[...] = acc[:, :cols].astype(BF)
        sib_ref[...] = acc[:, cols:].astype(BF)


def d_attn_kernel(video_ref, text_ref, gate_ref, w_ref, out_ref, d_out):
    @pl.when(pl.program_id(0) == 0)
    def _():
        vrows = video_ref.shape[0]
        d_out[0:vrows, :] = (video_ref[...].astype(F) * gate_ref[...]).astype(BF)
        d_out[vrows:, :] = (text_ref[...].astype(F) * gate_ref[...]).astype(BF)

    got = lax.dot_general(d_out[...], w_ref[...], NT, preferred_element_type=F)
    for j in range(out_ref.shape[0]):
        out_ref[j] = got[:, j * HD : (j + 1) * HD].astype(BF)


def out_kernel(attn_ref, w_ref, video_ref, text_ref, dv_ref, dt_ref, gate_ref, ov_ref, ot_ref, dg_ref, tok):
    rows = tok.shape[0]

    @pl.when(pl.program_id(0) == 0)
    def _():
        for j in range(attn_ref.shape[0]):
            tok[:, j * HD : (j + 1) * HD] = attn_ref[j, 0:rows, :]

    out = jnp.dot(tok[...], w_ref[...], preferred_element_type=F)
    vrows = video_ref.shape[0]
    top, low = out[:vrows], out[vrows:]
    gate = gate_ref[...]
    ov_ref[...] = (video_ref[...].astype(F) + gate * top).astype(BF)
    ot_ref[...] = (text_ref[...].astype(F) + gate * low).astype(BF)
    dg_ref[...] = jnp.sum(dv_ref[...].astype(F) * top, axis=0, keepdims=True) + jnp.sum(
        dt_ref[...].astype(F) * low, axis=0, keepdims=True
    )


def far_kernel(cut, own_ref, sib_ref, wo_ref, ws_ref, yct_ref, ycl_ref, m1_ref, m2_ref, m_ref, sum_ref):
    d = jnp.concatenate([own_ref[...], sib_ref[...]], axis=1)
    w = side_by_side(wo_ref, ws_ref)
    got = lax.dot_general(d, w, NT, preferred_element_type=F)
    rows = got.shape[0] // 4
    sum_ref[...] = jnp.sum(got, axis=0, keepdims=True)
    c, ya, yb, yc = (got[i * rows : (i + 1) * rows] for i in range(4))
    yct_ref[...] = yc[:cut].astype(BF)
    ycl_ref[...] = yc[cut:].astype(BF)
    m1_ref[...] = jnp.concatenate([ya[:cut], c[:cut]], axis=0).astype(BF)
    m2_ref[...] = jnp.concatenate([yb[cut:], c[cut:]], axis=0).astype(BF)
    m_ref[...] = jnp.concatenate([ya[cut:], yb[:cut]], axis=0).astype(BF)


def add_kernel(one_ref, two_ref, got1_ref, got2_ref, out1_ref, out2_ref):
    for base_ref, got_ref, out_ref in ((one_ref, got1_ref, out1_ref), (two_ref, got2_ref, out2_ref)):
        n = got_ref.shape[0]
        out_ref[:n, :] = (base_ref[:n, :].astype(F) + got_ref[...].astype(F)).astype(BF)
        out_ref[n:, :] = base_ref[n:, :]


def sums_kernel(cut, y_ref, a_ref, b_ref, r1_ref, r2_ref, r3_ref, oy_ref, oa_ref, ob_ref):
    part = y_ref.shape[0] - cut
    r1, r2, r3 = (ref[...].astype(F) for ref in (r1_ref, r2_ref, r3_ref))
    parts = (
        (y_ref, oy_ref, r1[:cut], r2[:part]),
        (a_ref, oa_ref, r1[cut:], r3[:part]),
        (b_ref, ob_ref, r3[part:], r2[part:]),
    )
    for ref, out, top, low in parts:
        out[...] = (ref[...].astype(F) + jnp.concatenate([top, low], axis=0)).astype(BF)


def near_kernel(own_ref, sib_ref, wo_ref, ws_ref, o_ref, y_ref, a_ref, b_ref, sum_ref):
    d = jnp.concatenate([own_ref[...], sib_ref[...]], axis=1)
    w = side_by_side(wo_ref, ws_ref)
    got = lax.dot_general(d, w, NT, preferred_element_type=F)
    rows = got.shape[0] // 4
    sum_ref[...] = jnp.sum(got, axis=0, keepdims=True)
    for i, ref in enumerate((o_ref, y_ref, a_ref, b_ref)):
        ref[...] = got[i * rows : (i + 1) * rows].astype(BF)


def grad_w_kernel(
    place_ref, one_ref, two_ref, own_ref, sib_ref, wo_ref, ws_ref, mod_ref, own_out, sib_out, m_ref, total,
):
    d = jnp.concatenate([own_ref[...], sib_ref[...]], axis=1)

    @pl.when(pl.program_id(0) == 0)
    def _():
        total[...] = jnp.sum(d.astype(F), axis=0, keepdims=True)

    normed = jnp.concatenate([one_ref[...], two_ref[...]], axis=0)
    got = lax.dot_general(normed, d, TN, preferred_element_type=F)
    w = side_by_side(wo_ref, ws_ref).astype(F)
    prod = got * w
    m_ref[...] = sum(prod[:, j : j + HD] for j in range(0, prod.shape[1], HD))
    rows = jnp.concatenate([mod_ref[...], jnp.zeros((5, mod_ref.shape[1]), F)], axis=0)
    columns = jnp.transpose(rows)
    got = got * (1.0 + columns[:, 1:2]) + columns[:, 0:1] * total[...]
    wide, cols = own_out.shape[3], own_ref.shape[1]
    count = normed.shape[1] // wide
    for i in range(count):
        at = (lax.rem(pl.program_id(0) * count, 4) + i - place_ref[0]) % 4
        for j in range(3):
            piece = got[i * wide : (i + 1) * wide]
            own_out[at, 0, j] = piece[:, j * HD : (j + 1) * HD].astype(BF)
            sib_out[at, 0, j] = piece[:, cols + j * HD : cols + (j + 1) * HD].astype(BF)


def gain_terms(values):
    high = values.astype(BF).astype(F)
    mid = (values - high).astype(BF).astype(F)
    low = values - high - mid
    pad = jnp.zeros((2, HD), F)
    return jnp.concatenate([high, mid, low, pad], axis=0).astype(BF)


def gain_value(terms):
    terms = terms.astype(F)
    return terms[0:2] + terms[2:4] + terms[4:6]


def both(own_ref, got_ref, k):
    total = own_ref[0, k].astype(F) + got_ref[0, k].astype(F)
    return total.reshape(total.shape[0] * total.shape[1], total.shape[2])


def far_section_kernel(own_ref, got_ref, attn_ref, f0_ref, f1_ref, gain_ref):
    flat = f0_ref.shape[0] - 8
    gains = gain_value(jnp.sum(attn_ref[...].astype(F), axis=0))
    for k, ref in enumerate((f0_ref, f1_ref)):
        ref[0:flat, :] = both(own_ref, got_ref, k).astype(BF)
        ref[flat:, :] = gain_terms(gains)
    gain_ref[...] = gains


def near_section_kernel(ao_ref, ag_ref, bo_ref, bg_ref, ga_ref, gb_ref, gain_ref, sa_ref, sb_ref, sum_ref):
    flat = ga_ref.shape[0] - 8
    sa_ref[0:flat, :] = both(ao_ref, ag_ref, 0).astype(BF)
    sa_ref[flat : 2 * flat, :] = (both(ao_ref, ag_ref, 1) + ga_ref[0:flat, :].astype(F)).astype(BF)
    sa_ref[2 * flat :, :] = ga_ref[flat:, :]
    sb_ref[0:flat, :] = (both(bo_ref, bg_ref, 0) + gb_ref[0:flat, :].astype(F)).astype(BF)
    sb_ref[flat:, :] = both(bo_ref, bg_ref, 1).astype(BF)
    sum_ref[...] = gain_ref[...] + gain_value(ga_ref[flat:, :]) + gain_value(gb_ref[flat:, :])


def own_section_kernel(own_ref, got_ref, a_ref, b_ref, gain_ref, keep_ref, give_ref, sum_ref):
    flat = keep_ref.shape[0]
    keep = both(own_ref, got_ref, 0)
    give = both(own_ref, got_ref, 1)
    keep_ref[...] = keep + a_ref[0:flat, :].astype(F) + b_ref[0:flat, :].astype(F)
    give += a_ref[flat : 2 * flat, :].astype(F) + b_ref[flat : 2 * flat, :].astype(F)
    give_ref[0:flat, :] = give.astype(BF)
    gains = gain_ref[...] + gain_value(a_ref[2 * flat :, :])
    give_ref[flat:, :] = gain_terms(gains)
    sum_ref[...] = gains


def tail_kernel(o_ref, ra_ref, rb_ref, ry_ref, video_ref, text_ref, dv_ref, dt_ref, mod_ref, gv_ref, gt_ref):
    scale = 1.0 + mod_ref[1:2, :]
    vrows = video_ref.shape[0]
    pieces = [(i, 16, video_ref, dv_ref, gv_ref, i) for i in range(0, vrows, 16)]
    pieces.append((vrows, text_ref.shape[0], text_ref, dt_ref, gt_ref, 0))
    for at, n, x_ref, dy_ref, g_ref, lo in pieces:
        d_h = sum(ref[at : at + n, :].astype(F) for ref in (o_ref, ra_ref, rb_ref, ry_ref))
        normed, rstd = layer_norm(x_ref[lo : lo + n, :].astype(F))
        t = d_h * scale
        back = rstd * (
            t
            - jnp.mean(t, axis=-1, keepdims=True)
            - normed * jnp.mean(t * normed, axis=-1, keepdims=True)
        )
        g_ref[lo : lo + n, :] = (dy_ref[lo : lo + n, :].astype(F) + back).astype(BF)


def rms(x):
    r = lax.rsqrt(jnp.mean(x * x, axis=-1, keepdims=True) + 1e-6)
    return x * r, r


def rms_back(t, xh, r):
    return r * (t - xh * jnp.mean(t * xh, axis=-1, keepdims=True))


def attn_kernel(
    rows, order_ref, q1_ref, q2_ref, s1_ref, s2_ref, bias_ref, do_ref, gq_ref, gk_ref,
    attn_ref, own_ref, give_ref, q_s, kn_s, v_s, dq_s, dk_s, dv_s, gain_s,
):
    part = q1_ref.shape[0]
    block = 2 * part
    parts = (q1_ref, q2_ref, s1_ref, s2_ref)
    outs = ((own_ref, 0), (own_ref, part), (give_ref, 0), (give_ref, part))
    per = block // rows
    scale = HD**-0.5
    step = pl.program_id(0)
    gq, gk = gq_ref[...], gk_ref[...]

    @pl.when(step == 0)
    def _():
        for i, ref in enumerate(parts):
            at = slice(i * part, (i + 1) * part)
            q_s[at, :] = ref[:, 0:HD]
            xh, _ = rms(ref[:, HD : 2 * HD].astype(F))
            kn_s[at, :] = (xh * gk).astype(BF)
            v_s[at, :] = ref[:, 2 * HD : 3 * HD]
        dk_s[...] = jnp.zeros_like(dk_s)
        dv_s[...] = jnp.zeros_like(dv_s)
        gain_s[...] = jnp.zeros_like(gain_s)

    here = pl.ds(pl.multiple_of(step * block, 16), block)
    xh, r = rms(q_s[here, :].astype(F))
    qn = (xh * (gq * scale)).astype(BF)
    s = lax.dot_general(qn, kn_s[...], NT, preferred_element_type=F) + bias_ref[...]
    e = jnp.exp(s)
    linv = 1.0 / jnp.sum(e, axis=-1, keepdims=True)
    eb = e.astype(BF)
    o = jnp.dot(eb, v_s[...], preferred_element_type=F) * linv
    do = jnp.concatenate(
        [do_ref[order_ref[step * per + j]].astype(F) for j in range(per)], axis=0
    )
    for j in range(per):
        attn_ref[order_ref[step * per + j], 0:rows, :] = o[j * rows : (j + 1) * rows].astype(BF)
    dn = do * linv
    dnb = dn.astype(BF)
    delta = jnp.sum(dn * o, axis=-1, keepdims=True)
    dp = lax.dot_general(dnb, v_s[...], NT, preferred_element_type=F)
    ds = (e * (dp - delta)).astype(BF)
    dq = jnp.dot(ds, kn_s[...], preferred_element_type=F)
    dk_s[...] += lax.dot_general(ds, qn, TN, preferred_element_type=F)
    dv_s[...] += lax.dot_general(eb, dnb, TN, preferred_element_type=F)
    gain_s[0:1, :] += jnp.sum(dq * xh, axis=0, keepdims=True) * scale
    dq_s[here, :] = rms_back(dq * (gq * scale), xh, r).astype(BF)

    @pl.when(step == 1)
    def _():
        for i, ref in enumerate(parts):
            out, at = outs[i]
            out[at : at + part, 0:HD] = dq_s[i * part : (i + 1) * part, :]
            xh, r = rms(ref[:, HD : 2 * HD].astype(F))
            dk = dk_s[i * part : (i + 1) * part, :]
            gain_s[1:2, :] += jnp.sum(dk * xh, axis=0, keepdims=True)
            out[at : at + part, HD : 2 * HD] = rms_back(dk * gk, xh, r).astype(BF)
            out[at : at + part, 2 * HD :] = dv_s[i * part : (i + 1) * part, :].astype(BF)
        gains = gain_s[...]
        high = gains.astype(BF).astype(F)
        low = (gains - high).astype(BF).astype(F)
        rest = gains - high - low
        tail = jnp.concatenate([high[0:2], low[0:2], rest[0:2], jnp.zeros((2, HD), F)], axis=0)
        attn_ref[:, rows:, :] = jnp.broadcast_to(tail.astype(BF)[None], (attn_ref.shape[0], 8, HD))


def ring(values, axis, distance):
    size = lax.axis_size(axis)
    return lax.ppermute(values, axis, [(i, (i + distance) % size) for i in range(size)])


def tie(values, *after):
    return lax.optimization_barrier((values, *after))[0]


def per_device(
    video, text, prompt_len, modulation, q_gain, k_gain, w_qkv, w_out, cot_video, cot_text
):
    video, text, cot_video, cot_text, modulation = (
        a[0] for a in (video, text, cot_video, cot_text, modulation)
    )
    vrows, trows = video.shape[0], text.shape[0]
    rows, width = vrows + trows, video.shape[1]
    heads = w_out.shape[0] // HD
    cols = 3 * HD
    yi, zi, ci = (lax.axis_index(a) for a in SEQ)
    zp = functools.partial(ring, axis="z", distance=1)
    zm = functools.partial(ring, axis="z", distance=-1)
    yy = functools.partial(ring, axis="y", distance=1)
    cc = functools.partial(ring, axis="core", distance=1)
    gate = modulation[2:3]
    cut = 64
    part = rows - cut

    h = call(norm_kernel, shape((rows, width)))(video, text)
    w_own = jnp.transpose(w_qkv, (1, 0, 2))
    step = 2 * HD
    per = 4

    w_sib = cc(w_own)
    h_a, h_b, h_y = zp(h), zm(h), yy(h)
    d_attn = call(
        d_attn_kernel,
        shape((heads, rows, HD)),
        grid=(2 * per,),
        in_specs=[
            whole((vrows, width)),
            whole((trows, width)),
            whole((1, width)),
            pl.BlockSpec((step, width), lambda i: (i, 0)),
        ],
        out_specs=pl.BlockSpec((step // HD, rows, HD), lambda i: (i, 0, 0)),
        scratch_shapes=[pltpu.VMEM((rows, width), BF)],
    )(cot_video, cot_text, tie(gate, h, w_sib), w_out)
    y_t, y_l, a_t, b_l, m_ab = call(
        functools.partial(split_kernel, cut), tuple(shape((k, width)) for k in (cut, part, cut, part, rows))
    )(tie(h_y, d_attn), h_a, h_b)
    ya_t, yb_l = zp(y_t), zm(y_l)
    c_t, c_l = zp(a_t), zm(b_l)
    m_ab = yy(m_ab)
    n = len(PLACES) * rows
    block = n // 2
    strip = 1024

    def project(us, *parts):
        return call(
            functools.partial(qkv_kernel, len(parts)),
            (shape((block, width)), shape((block, cols)), shape((block, cols))),
            mib=56,
            us=us,
            grid=(width // strip,),
            in_specs=[pl.BlockSpec((k.shape[0], strip), lambda i: (0, i)) for k in parts]
            + [pl.BlockSpec((3, strip, HD), lambda i: (0, i, 0))] * 2
            + [pl.BlockSpec((3, strip), lambda i: (0, i))],
            out_specs=[
                pl.BlockSpec((block, strip), lambda i: (0, i)),
                whole((block, cols)),
                whole((block, cols)),
            ],
            scratch_shapes=[pltpu.VMEM((block, 2 * cols), F)],
        )(*parts, w_own, w_sib, modulation)

    h_one, own_one, sib_one = project(0, h, h_y, h_a, h_b)
    yc_t, yc_l = zp(tie(ya_t, own_one)), zm(tie(yb_l, own_one))
    d_heads = lax.all_to_all(
        tie(d_attn, yc_t, yc_l), SEQ, split_axis=0, concat_axis=0, tiled=True
    )
    h_two, own_two, sib_two = project(0, c_t, c_l, ya_t, m_ab, yb_l, yc_t, yc_l)
    sib_two = cc(sib_two)
    sib_one = cc(tie(sib_one, own_two))

    order = jnp.stack(
        [(((yi + a) % 2) * 4 + (zi + b) % 4) * 2 + (ci + k) % 2 for k in (0, 1) for a, b in PLACES]
    ).astype(jnp.int32)
    inner = jnp.arange(rows, dtype=jnp.int32)[None, :]
    valid = (inner < vrows) | (order[:, None] * trows + inner - vrows < prompt_len[0])
    bias = jnp.where(valid, 0.0, -1e30).astype(F).reshape(1, 2 * n)

    attn, d_own, d_give = call(
        functools.partial(attn_kernel, rows),
        (shape((heads, rows + 8, HD)), shape((n, cols)), shape((n, cols))),
        mib=56,
        grid_spec=pltpu.PrefetchScalarGridSpec(
            num_scalar_prefetch=1,
            grid=(2,),
            in_specs=[whole(a) for a in ((block, cols),) * 4]
            + [whole((1, 2 * n)), whole((heads, rows, HD)), whole((1, HD)), whole((1, HD))],
            out_specs=[whole((heads, rows + 8, HD)), whole((n, cols)), whole((n, cols))],
            scratch_shapes=[
                pltpu.VMEM((2 * n, HD), BF),
                pltpu.VMEM((2 * n, HD), BF),
                pltpu.VMEM((2 * n, HD), BF),
                pltpu.VMEM((2 * n, HD), BF),
                pltpu.VMEM((2 * n, HD), F),
                pltpu.VMEM((2 * n, HD), F),
                pltpu.VMEM((8, HD), F),
            ],
        ),
    )(order, own_one, own_two, sib_one, sib_two, bias, d_heads, q_gain[None], k_gain[None])

    d_sib = cc(d_give)

    xi, hi = lax.axis_index("x"), lax.axis_index("yh")
    wide = width // 8
    here = jnp.stack([xi - 4, hi - 2]).astype(jnp.int32)

    attn_tok = lax.all_to_all(attn, SEQ, split_axis=0, concat_axis=0, tiled=True)
    strips = lambda count: pl.BlockSpec((count, strip), lambda i: (0, i))
    sizes = (cut, part, 2 * cut, 2 * part, rows)
    half_specs = lambda at: [
        pl.BlockSpec((block, cols), lambda i: (at, 0)),
        pl.BlockSpec((block, cols), lambda i: (at, 0)),
        pl.BlockSpec((3, strip, HD), lambda i: (0, i, 0)),
        pl.BlockSpec((3, strip, HD), lambda i: (0, i, 0)),
    ]
    work = dict(grid=(width // strip,), mib=56)
    yc_t, yc_l, m_1, m_2, m_3, far_sum = call(
        functools.partial(far_kernel, cut),
        tuple(shape((k, width)) for k in sizes) + (shape((1, width), F),),
        in_specs=half_specs(1),
        out_specs=[strips(k) for k in sizes + (1,)],
        **work,
    )(d_own, d_sib, w_own, w_sib)
    r_ya, r_yb = zm(yc_t), zp(yc_l)
    r_3 = yy(m_3)
    g_own, g_sib, mod_sums = call(
        grad_w_kernel,
        (shape((4, 2, 3, wide, HD)),) * 2 + (shape((width, HD), F),),
        us=20,
        mib=56,
        grid_spec=pltpu.PrefetchScalarGridSpec(
            num_scalar_prefetch=1,
            grid=(4,),
            in_specs=[pl.BlockSpec((block, 2 * wide), lambda i, p: (0, i))] * 2
            + [whole((n, cols))] * 2
            + [pl.BlockSpec((3, 2 * wide, HD), lambda i, p: (0, i, 0))] * 2
            + [pl.BlockSpec((3, 2 * wide), lambda i, p: (0, i))],
            out_specs=[
                pl.BlockSpec((4, 1, 3, wide, HD), lambda i, p: (0, (i // 2 - p[1]) % 2, 0, 0, 0))
            ]
            * 2
            + [pl.BlockSpec((2 * wide, HD), lambda i, p: (i, 0))],
            scratch_shapes=[pltpu.VMEM((1, 2 * cols), F)],
        ),
    )(tie(here, m_3), h_one, h_two, d_own, d_sib, w_own, w_sib, modulation)


    thirds = lambda count: pl.BlockSpec((count, width // 3), lambda i: (0, i))

    m_1, m_2 = call(
        add_kernel,
        (shape((2 * cut, width)), shape((2 * part, width))),
        us=30,
        grid=(3,),
        in_specs=[thirds(k) for k in (2 * cut, 2 * part, cut, part)],
        out_specs=[thirds(2 * cut), thirds(2 * part)],
    )(tie(m_1, g_own), m_2, r_ya, r_yb)
    r_1, r_2 = zm(m_1), zp(m_2)
    g_got = cc(g_sib)
    flat = 3 * wide
    pick = lambda r: [pl.BlockSpec((1, 2, 3, wide, HD), lambda i: (r, 0, 0, 0, 0))] * 2
    two = shape((2, HD), F)
    far_0, far_1, gains = call(
        far_section_kernel,
        (shape((flat + 8, HD)), shape((flat + 8, HD)), two),
        grid=(1,),
        in_specs=pick(2) + [pl.BlockSpec((heads, 8, HD), lambda i: (0, rows // 8, 0))],
        out_specs=[whole((flat + 8, HD)), whole((flat + 8, HD)), whole((2, HD))],
    )(g_own, g_got, tie(attn_tok, m_1, m_2))
    got_b, got_a = ring(far_0, "x", -1), ring(far_1, "x", 1)
    p_o, p_y, p_a, p_b, near_sum = call(
        near_kernel,
        (shape((rows, width)),) * 4 + (shape((1, width), F),),
        in_specs=half_specs(0),
        out_specs=[strips(rows)] * 4 + [strips(1)],
        us=30,
        **work,
    )(tie(d_own, m_3, far_0), d_sib, w_own, w_sib)
    send_a, send_b, gains = call(
        near_section_kernel,
        (shape((2 * flat + 8, HD)), shape((2 * flat, HD)), two),
        grid=(1,),
        in_specs=pick(1) + pick(3) + [whole((flat + 8, HD))] * 2 + [whole((2, HD))],
        out_specs=[whole((2 * flat + 8, HD)), whole((2 * flat, HD)), whole((2, HD))],
    )(g_own, g_got, g_own, g_got, got_a, got_b, tie(gains, p_o))
    p_y, p_a, p_b = call(
        functools.partial(sums_kernel, cut),
        (shape((rows, width)),) * 3,
        grid=(3,),
        in_specs=[thirds(k) for k in (rows, rows, rows, 2 * cut, 2 * part, rows)],
        out_specs=[thirds(rows)] * 3,
    )(
        tie(p_y, send_a, send_b), p_a, p_b, r_1, r_2, r_3
    )
    last_a, last_b, last_y = zm(p_a), zp(p_b), yy(p_y)

    back_a, back_b = ring(send_a, "x", 1), ring(send_b, "x", -1)
    keep, give, gains = call(
        own_section_kernel,
        (shape((flat, HD), F), shape((flat + 8, HD)), two),
        grid=(1,),
        in_specs=pick(0) + [whole((2 * flat + 8, HD)), whole((2 * flat, HD)), whole((2, HD))],
        out_specs=[whole((flat, HD)), whole((flat + 8, HD)), whole((2, HD))],
    )(g_own, g_got, back_a, back_b, gains)
    got = ring(give, "yh", 1)
    grad_w = (keep + got[:flat].astype(F)).reshape(3, wide, HD)
    grad_w = jnp.transpose(grad_w, (1, 0, 2))
    last = got[flat:].astype(F)
    grad_gain = gains + last[0:2] + last[2:4] + last[4:6]

    out_video, out_text, d_gate = call(
        out_kernel,
        (shape((vrows, width)), shape((trows, width)), shape((1, width), F)),
        us=8,
        grid=(width // strip,),
        mib=56,
        in_specs=[
            whole((heads, rows + 8, HD)),
            pl.BlockSpec((heads * HD, strip), lambda i: (0, i)),
        ]
        + [strips(k) for k in (vrows, trows, vrows, trows, 1)],
        out_specs=[strips(k) for k in (vrows, trows, 1)],
        scratch_shapes=[pltpu.VMEM((rows, heads * HD), BF)],
    )(tie(attn_tok, p_y), w_out, video, text, cot_video, cot_text, gate)

    mod_sums = jnp.sum(tie(mod_sums, p_y), axis=1)[None]
    mod_sums = jnp.concatenate([far_sum + near_sum, mod_sums, d_gate], axis=0).astype(BF)
    wide_mod = jnp.broadcast_to(mod_sums[None], (heads,) + mod_sums.shape)
    grad_video, grad_text = call(
        tail_kernel,
        (shape((vrows, width)), shape((trows, width))),
    )(tie(p_o, give), last_a, last_b, last_y, video, text, cot_video, cot_text, modulation)
    grad_mod = jnp.sum(
        tie(
            lax.all_to_all(wide_mod, SEQ, split_axis=0, concat_axis=0, tiled=True), grad_video
        ).astype(F),
        axis=0,
    )
    return (
        out_video[None],
        out_text[None],
        grad_video[None],
        grad_text[None],
        grad_mod[None],
        grad_w,
        grad_gain,
    )


def solution(mesh):
    fine = Mesh(mesh.devices.reshape(2, 4, 2, 4, 2), EVERY)
    tokens = P(SECTION, SEQ, None)
    sample = P(SECTION, None, None)
    return jax.shard_map(
        per_device,
        mesh=fine,
        in_specs=(tokens, tokens, P(SECTION), sample, P(), P(), P(None, None, SEQ), P(), tokens, tokens),
        out_specs=(tokens, tokens, tokens, tokens, sample, P(SECTION, None, SEQ), P()),
        check_vma=False,
    )
```
